32 devices in a mesh: rows: 4 (over x, core), cols: 8 (over z, y).
Axes of the slice: x: 2, y: 2, z: 4, core: 2. Of those that a mesh axis runs over, the one named last changes fastest.
Arguments:
- low_feats: bfloat16 [64, 256, 256], P('rows', 'cols'), may hold values from -6 to 6
- skip_feats: bfloat16 [128, 512, 256], P('rows', 'cols'), may hold values from -6 to 6
- tissue_mask: int32 [32, 128], P('rows', 'cols'), may hold values 0 or 1
- owner_slot: int32 [32, 128], P('rows', 'cols'), may hold values from 0 to 4095, as said below
- filter_one: bfloat16 [32, 3, 3, 256], replicated, may hold values from -0.125 to 0.125
- filter_two: bfloat16 [32, 3, 3, 256], replicated, may hold values from -0.125 to 0.125
- out_grad: bfloat16 [128, 512, 256], P('rows', 'cols'), may hold values from -6 to 6
Outputs:
- output: bfloat16 [128, 512, 256], P('rows', 'cols')
- skip_grad: bfloat16 [4096, 4, 4, 256], P(('rows', 'cols'))
- low_grad: bfloat16 [64, 256, 256], P('rows', 'cols')
- filter_grad_one: float32 [32, 3, 3, 256], replicated
- filter_grad_two: float32 [32, 3, 3, 256], replicated
The draws below stay inside these ranges and needn't reach their ends.
Inputs may be any that keep to these rules, and one draw needn't show every extreme that they name: `owner_slot`: all values are distinct, so every encoder slot receives exactly one tile: each owner gets exactly 128 tiles. At most 8 tiles of one device go to one owner, and every device sends exactly 8 tiles to some owner.
All inputs are finite; a program needn't handle non-finite values. No bound on the sum of `tissue_mask` on one device may be relied on, other than what follows from the above.
Results may differ from the reference program's by a relative error of at most 0.006.
Values may be sent and summed in bfloat16 or wider, within the bound.
A program may use at most 128 MiB of HBM per device.

```python
import math
import jax
import jax.numpy as jnp
import numpy as np
from jax import lax

C = 32
G = 8
P_SIZE = 4
TR = 8
TC = 16
TILES_DEV = 128
OWNERS = 32
CAP = 8
NTR = 32
NTC = 128
HEIGHT = 128
BREADTH = 512
FEAT = 256
ENC_TILES = 4096
N_ROWS = 4
N_COLS = 8


def draw_owner_slot(key, part):
    key_count, key_order, key_source, key_owner, key_tiles = jax.random.split(key, 5)
    half = CAP // 2
    heavy = jax.random.randint(key_count, (), 1, OWNERS // 2 + 1)
    order = jax.random.permutation(key_order, OWNERS)
    position = jnp.zeros((OWNERS,), jnp.int32).at[order].set(jnp.arange(OWNERS, dtype=jnp.int32))
    counts = jnp.where(position < heavy, CAP, jnp.where(position < 2 * heavy, 0, half)).astype(jnp.int32)
    ends = jnp.cumsum(counts)
    slot_ids = jnp.arange(TILES_DEV, dtype=jnp.int32)
    group_of = jnp.sum((ends[None, :] <= slot_ids[:, None]).astype(jnp.int32), axis=1)
    source_shift = jax.random.permutation(key_source, OWNERS)
    owner_order = jax.random.permutation(key_owner, OWNERS)
    tile_keys = jax.random.split(key_tiles, OWNERS)
    shuffled = jax.vmap(lambda one_key: jax.random.permutation(one_key, TILES_DEV))(tile_keys)
    groups = group_of[shuffled]
    owner = owner_order[(source_shift[:, None] + groups) % OWNERS]
    flat_slot = owner * TILES_DEV + shuffled
    laid = flat_slot.reshape(N_ROWS, N_COLS, TR, TC).transpose(0, 2, 1, 3)
    return laid.reshape(N_ROWS * TR, N_COLS * TC).astype(jnp.int32)


def set_ends(entries, key, smallest, high):
    place = [jax.random.randint(jax.random.fold_in(key, axis), (), 0, length) for axis, length in enumerate(entries.shape)]
    widest = entries.shape.index(max(entries.shape))
    next_to = place[:widest] + [(place[widest] + 1) % entries.shape[widest]] + place[widest + 1:]
    return entries.at[tuple(place)].set(smallest).at[tuple(next_to)].set(high)


def steps_of(key, shape, cuts, least, top_value):
    gain, own = 1.0, jax.random.fold_in(key, 6)
    for axis_at, blocks in cuts:
        heights = jnp.exp(jax.random.uniform(jax.random.fold_in(own, axis_at), (blocks,), jnp.float32, least / len(cuts), top_value / len(cuts)))
        gain = gain * jnp.repeat(heights, shape[axis_at] // blocks).reshape([-1 if axis == axis_at else 1 for axis in range(len(shape))])
    return gain


def centred(stream_key, shape, deviation, limit, pieces=(), kind=jnp.bfloat16):
    level = steps_of(stream_key, shape, pieces, -0.22, 0.18) if pieces else 1.0
    entries = jax.random.normal(stream_key, shape, jnp.float32) * deviation * level
    return jnp.minimum(jnp.maximum(entries, -limit), limit).astype(kind)


def setup_inputs(seed: int = 0) -> dict:
    key_of = jax.random.split(jax.random.key(seed), 8)
    return {
        "low_feats": centred(key_of[0], (HEIGHT // 2, BREADTH // 2, FEAT), 1.0, 6.0, ((0, 4), (1, 8))),
        "skip_feats": centred(key_of[1], (HEIGHT, BREADTH, FEAT), 1.0, 6.0, ((0, 4), (1, 8))),
        "tissue_mask": set_ends((jax.random.randint(key_of[2], (NTR, NTC), 0, 4) < 3).astype(jnp.int32), jax.random.fold_in(key_of[2], 1), 0, 1),
        "owner_slot": draw_owner_slot(jax.random.fold_in(key_of[7], 71), 0),
        "filter_one": centred(key_of[4], (C, 3, 3, FEAT), (9 * FEAT) ** -0.5, 0.125),
        "filter_two": centred(key_of[5], (C, 3, 3, FEAT), (9 * FEAT) ** -0.5, 0.125),
        "out_grad": centred(key_of[6], (HEIGHT, BREADTH, FEAT), 1.0, 6.0, ((0, 4), (1, 8))),
    }


def element_inverse(element):
    mirror = element // 4
    turns = element % 4
    return np.where(mirror == 0, (4 - turns) % 4, element)

def element_product(first, second):
    mirror = (first // 4 + second // 4) % 2
    turns = (first % 4 + (1 - 2 * (first // 4)) * (second % 4)) % 4
    return mirror * 4 + turns

def element_act(element, row_off, col_off):
    mirror = element // 4
    turns = element % 4
    col_now = np.where(mirror == 1, -col_off, col_off)
    row_now = row_off
    for step in range(3):
        rotated_row = -col_now
        rotated_col = row_now
        row_now = np.where(turns > step, rotated_row, row_now)
        col_now = np.where(turns > step, rotated_col, col_now)
    return (row_now, col_now)

def group_index(channels):
    features = channels * G
    row_in, col_in, feat_in, out_chan, out_elem = np.meshgrid(np.arange(3), np.arange(3), np.arange(features), np.arange(channels), np.arange(G), indexing='ij')
    inverse = element_inverse(out_elem)
    moved_row, moved_col = element_act(inverse, row_in - 1, col_in - 1)
    moved_elem = element_product(inverse, feat_in % G)
    flat_index = ((out_chan * 3 + moved_row + 1) * 3 + moved_col + 1) * features + feat_in // G * G + moved_elem
    return flat_index.reshape(3, 3, features, features).astype(np.int32)

def expand(base):
    channels = base.shape[0]
    features = base.shape[3]
    table = jnp.asarray(group_index(channels).reshape(-1))
    return base.reshape(-1)[table].reshape(3, 3, features, features)

def fold_filter(grad_full, channels):
    features = channels * G
    table = jnp.asarray(group_index(channels).reshape(-1))
    summed = jax.ops.segment_sum(grad_full.reshape(-1), table, num_segments=channels * 9 * features)
    return summed.reshape(channels, 3, 3, features)

def pad_cycle(field):
    return jnp.pad(field, ((1, 1), (1, 1), (0, 0)))

def conv_valid(padded, kernel):
    result = lax.conv_general_dilated(padded[None].astype(jnp.float32), kernel.astype(jnp.float32), (1, 1), 'VALID', dimension_numbers=('NHWC', 'HWIO', 'NHWC'), precision=lax.Precision.HIGHEST)
    return result[0]

def flipped(kernel):
    return jnp.flip(kernel, (0, 1)).transpose(0, 1, 3, 2)

def filter_terms(padded, grad_out):
    height = grad_out.shape[0]
    breadth = grad_out.shape[1]
    flat_grad = grad_out.reshape(-1, grad_out.shape[2]).astype(jnp.float32)
    stacked = []
    for row_off in range(3):
        for col_off in range(3):
            window = padded[row_off:row_off + height, col_off:col_off + breadth].reshape(-1, padded.shape[2]).astype(jnp.float32)
            stacked.append(lax.dot_general(window, flat_grad, (((0,), (0,)), ((), ())), precision=lax.Precision.HIGHEST, preferred_element_type=jnp.float32))
    return jnp.stack(stacked).reshape(3, 3, padded.shape[2], grad_out.shape[2])

def silu_slope(value):
    sigma = jax.nn.sigmoid(value)
    return sigma * (1.0 + value * (1.0 - sigma))

def reference(low_feats, skip_feats, tissue_mask, owner_slot, filter_one, filter_two, out_grad):
    pixel_mask = jnp.repeat(jnp.repeat(tissue_mask, P_SIZE, 0), P_SIZE, 1).astype(jnp.float32)[:, :, None]
    upsampled = jnp.repeat(jnp.repeat(low_feats, 2, 0), 2, 1).astype(jnp.float32)
    merged = ((upsampled + skip_feats.astype(jnp.float32)) * pixel_mask).astype(jnp.bfloat16)
    kernel_one = expand(filter_one)
    kernel_two = expand(filter_two)
    padded_merged = pad_cycle(merged)
    pre_one = conv_valid(padded_merged, kernel_one)
    hidden = (jax.nn.silu(pre_one) * pixel_mask).astype(jnp.bfloat16)
    padded_hidden = pad_cycle(hidden)
    output = (conv_valid(padded_hidden, kernel_two) * pixel_mask).astype(jnp.bfloat16)
    grad_two = (out_grad.astype(jnp.float32) * pixel_mask).astype(jnp.bfloat16)
    grad_hidden = conv_valid(pad_cycle(grad_two), flipped(kernel_two))
    grad_pre = (grad_hidden * silu_slope(pre_one) * pixel_mask).astype(jnp.bfloat16)
    grad_merged = conv_valid(pad_cycle(grad_pre), flipped(kernel_one)) * pixel_mask
    low_grad = grad_merged.reshape(HEIGHT // 2, 2, BREADTH // 2, 2, FEAT).sum(axis=(1, 3)).astype(jnp.bfloat16)
    skip_tiles = grad_merged.astype(jnp.bfloat16).reshape(NTR, P_SIZE, NTC, P_SIZE, FEAT).transpose(0, 2, 1, 3, 4).reshape(NTR * NTC, P_SIZE, P_SIZE, FEAT)
    skip_grad = jnp.zeros((ENC_TILES, P_SIZE, P_SIZE, FEAT), jnp.bfloat16).at[owner_slot.reshape(-1).astype(jnp.int32)].set(skip_tiles)
    scale = 1.0 / math.sqrt(HEIGHT * BREADTH)
    filter_grad_one = fold_filter(filter_terms(padded_merged, grad_pre), C) * scale
    filter_grad_two = fold_filter(filter_terms(padded_hidden, grad_two), C) * scale
    return (output, skip_grad, low_grad, filter_grad_one, filter_grad_two)
```

```python
import functools
import math

import jax
import jax.numpy as jnp
import numpy as np
from jax import lax
from jax.experimental import pallas as pl
from jax.experimental.pallas import tpu as pltpu
from jax.sharding import PartitionSpec as P

G = 8
MESH = pl.DeviceIdType.MESH
F32 = jnp.float32
BF16 = jnp.bfloat16
VMEM_BYTES = 56 * 1024 * 1024


def element_inverse(element):
    mirror, turns = element // 4, element % 4
    return element if mirror else (4 - turns) % 4


def element_product(first, second):
    mirror = (first // 4 + second // 4) % 2
    turns = (first % 4 + (1 - 2 * (first // 4)) * (second % 4)) % 4
    return mirror * 4 + turns


def element_act(element, row_off, col_off):
    mirror, turns = element // 4, element % 4
    row_now, col_now = row_off, -col_off if mirror else col_off
    for _ in range(turns):
        row_now, col_now = -col_now, row_now
    return row_now, col_now


def cell_source(element, cell):
    row, col = element_act(element_inverse(element), cell // 3 - 1, cell % 3 - 1)
    return (row + 1) * 3 + col + 1


def feature_moves(features):
    moves = np.zeros((G, features, features), np.float32)
    for elem in range(G):
        for i in range(features):
            moves[elem, i, i // G * G + element_product(element_inverse(elem), i % G)] = 1
    return moves


def element_major(features):
    channels = features // G
    order = np.zeros((features, features), np.float32)
    for o in range(channels):
        for g in range(G):
            order[g * channels + o, o * G + g] = 1
    return order


def tile_order(side, breadth):
    order = np.zeros((side * breadth, side * breadth), np.float32)
    for py in range(side):
        for x in range(breadth):
            order[(x // side * side + py) * side + x % side, py * breadth + x] = 1
    return order


def dot_nn(a, b):
    return lax.dot_general(a, b, (((1,), (0,)), ((), ())), preferred_element_type=F32)


def dot_nt(a, b):
    return lax.dot_general(a, b, (((1,), (1,)), ((), ())), preferred_element_type=F32)


def split(value):
    high = value.astype(BF16)
    return high, (value - high.astype(F32)).astype(BF16)


def shifted(row, left, right):
    breadth = row.shape[0]
    at = lax.broadcasted_iota(jnp.int32, row.shape, 0)
    before = jnp.where(at == 0, left, pltpu.roll(row, 1, 0))
    after = jnp.where(at == breadth - 1, right, pltpu.roll(row, breadth - 1, 0))
    return before.astype(BF16), after.astype(BF16)


def front_kernel(
    shape,
    low_ref, skip_ref, grad_ref, tissue_ref, base_ref, moves_ref, major_ref, tiling_ref, from_ref,
    send_ref, low_grad_ref, win_m_ref, win_h_ref, two_ref, pre_ref, lanes_ref, mask_ref,
    field, ends, wire, got_row, got_col, got_cor, win_g, win_p, gathered, rows_ref, tiles, halo32,
    send_sem, recv_sem,
):
    nr, nc = shape
    height, breadth, feats = skip_ref.shape
    tile_rows, tile_cols = tissue_ref.shape
    side = height // tile_rows
    chans = feats // G
    r, c = lax.axis_index("rows"), lax.axis_index("cols")
    up, down = lax.rem(r + nr - 1, nr), lax.rem(r + 1, nr)
    west, east = lax.rem(c + nc - 1, nc), lax.rem(c + 1, nc)
    around = ((up, c), (down, c), (r, west), (r, east), (up, west), (up, east), (down, west), (down, east))

    barrier = pltpu.get_barrier_semaphore()
    for device in around:
        pl.semaphore_signal(barrier, inc=1, device_id=device, device_id_type=MESH)

    spread = (
        lax.broadcasted_iota(jnp.int32, (breadth, tile_cols), 0) // side
        == lax.broadcasted_iota(jnp.int32, (breadth, tile_cols), 1)
    )
    ones = jnp.ones((tile_cols, feats), BF16)
    for tr in range(tile_rows):
        held = jnp.where(spread, tissue_ref[tr : tr + 1, :].astype(F32), 0.0).astype(BF16)
        mask_ref[tr] = dot_nn(held, ones)

    double = (
        lax.broadcasted_iota(jnp.int32, (breadth, breadth // 2), 0) // 2
        == lax.broadcasted_iota(jnp.int32, (breadth, breadth // 2), 1)
    ).astype(F32).astype(BF16)

    def enter(pair, _):
        raised = dot_nn(double, low_ref[pair])
        mask = mask_ref[pair * 2 // side]
        for k in range(2):
            y = pair * 2 + k
            merged = (raised + skip_ref[y].astype(F32)) * mask
            two = grad_ref[y].astype(F32) * mask
            field[0, 0, y] = merged.astype(BF16)
            field[0, 1, y] = two.astype(BF16)
            two_ref[y] = two.astype(BF16)
            for f, value in enumerate((merged, two)):
                ends[0, f, pl.ds(y, 1), :] = value[0:1]
                ends[1, f, pl.ds(y, 1), :] = value[breadth - 1 : breadth]
        return 0

    lax.fori_loop(0, height // 2, enter, 0)

    def copies(ph):
        low_end, high_end = pl.ds(0, 16), pl.ds(breadth - 16, 16)
        plan = (
            (field.at[ph, :, 0], got_row.at[ph, 1]),
            (field.at[ph, :, height - 1], got_row.at[ph, 0]),
            (wire.at[ph, 0], got_col.at[ph, 1]),
            (wire.at[ph, 1], got_col.at[ph, 0]),
            (field.at[ph, :, 0, low_end], got_cor.at[ph, 3]),
            (field.at[ph, :, 0, high_end], got_cor.at[ph, 2]),
            (field.at[ph, :, height - 1, low_end], got_cor.at[ph, 1]),
            (field.at[ph, :, height - 1, high_end], got_cor.at[ph, 0]),
        )
        return [
            pltpu.make_async_remote_copy(
                src_ref=src, dst_ref=dst, send_sem=send_sem.at[ph, k], recv_sem=recv_sem.at[ph, k],
                device_id=around[k], device_id_type=MESH,
            )
            for k, (src, dst) in enumerate(plan)
        ]

    def send_halo(ph):
        wire[ph] = ends[...].astype(BF16)
        started = copies(ph)
        for copy in started:
            copy.start()
        return started

    in_up = jnp.where(r > 0, 1.0, 0.0)
    in_down = jnp.where(r < nr - 1, 1.0, 0.0)
    in_west = jnp.where(c > 0, 1.0, 0.0)
    in_east = jnp.where(c < nc - 1, 1.0, 0.0)

    def windows(ph, f, out):
        halo32[0] = got_col[ph, 0, f].astype(F32) * in_west
        halo32[1] = got_col[ph, 1, f].astype(F32) * in_east

        def put(y, row, left, right):
            before, after = shifted(row, left, right)
            out[y, :, 0:feats] = before
            out[y, :, feats : 2 * feats] = row.astype(BF16)
            out[y, :, 2 * feats : 3 * feats] = after

        def inner(y, _):
            put(y + 1, field[ph, f, y].astype(F32), halo32[0, pl.ds(y, 1), :], halo32[1, pl.ds(y, 1), :])
            return 0

        lax.fori_loop(0, height, inner, 0)
        for k, (y, gate) in enumerate(((0, in_up), (height + 1, in_down))):
            row = got_row[ph, k, f].astype(F32) * gate
            left = got_cor[ph, 2 * k, f].astype(F32)[15:16] * (gate * in_west)
            right = got_cor[ph, 2 * k + 1, f].astype(F32)[0:1] * (gate * in_east)
            put(y, row, left, right)

    pl.semaphore_wait(barrier, 8)
    first = send_halo(0)

    def gather(g):
        placed = dot_nt(base_ref[...], moves_ref[g]).astype(BF16)
        for f in range(2):
            for cell in range(9):
                at = (f * 9 + cell_source(g, cell)) * chans
                gathered[f * 9 + cell, g * chans : (g + 1) * chans, :] = placed[at : at + chans]

    for g in range(G):
        gather(g)
    for f in range(2):
        for ky in range(3):
            for kx in range(3):
                full = lax.dot_general(
                    major_ref[...], gathered[f * 9 + ky * 3 + kx], (((0,), (0,)), ((), ())),
                    preferred_element_type=F32,
                ).astype(BF16)
                lanes_ref[f, ky, :, kx * feats : (kx + 1) * feats] = full
                rows_ref[f, 2 - ky, (2 - kx) * feats : (3 - kx) * feats, :] = full

    for copy in first:
        copy.wait()
    windows(0, 0, win_m_ref)
    windows(0, 1, win_g)

    step = 2 * side
    area = step * breadth

    def masked(y):
        two_rows = mask_ref[pl.ds(y // side, 2)]
        return jnp.broadcast_to(two_rows[:, None], (2, side, breadth, feats)).reshape(area, feats)

    def middle(i, _):
        y = i * step
        pre = jnp.zeros((area, feats), F32)
        back = jnp.zeros((area, feats), F32)
        for ky in range(3):
            pre += dot_nt(win_m_ref[pl.ds(y + ky, step)].reshape(area, 3 * feats), lanes_ref[0, ky])
            back += dot_nn(win_g[pl.ds(y + ky, step)].reshape(area, 3 * feats), rows_ref[1, ky])
        mask = masked(y)
        sigma = jax.nn.sigmoid(pre)
        hidden = (pre * sigma * mask).reshape(step, breadth, feats)
        slope = (back * (sigma * (1.0 + pre * (1.0 - sigma))) * mask).reshape(step, breadth, feats)
        for f, value in enumerate((hidden, slope)):
            field[1, f, pl.ds(y, step)] = value.astype(BF16)
            for k in range(step):
                ends[0, f, pl.ds(y + k, 1), :] = value[k, 0:1]
                ends[1, f, pl.ds(y + k, 1), :] = value[k, breadth - 1 : breadth]
        pre_ref[pl.ds(y, step)] = slope.astype(BF16)
        return 0

    lax.fori_loop(0, height // step, middle, 0)
    second = send_halo(1)
    for copy in second:
        copy.wait()
    windows(1, 1, win_p)

    halve = (
        lax.broadcasted_iota(jnp.int32, (breadth // 2, breadth), 1) // 2
        == lax.broadcasted_iota(jnp.int32, (breadth // 2, breadth), 0)
    ).astype(F32).astype(BF16)

    def last(i, _):
        y = i * step
        total = jnp.zeros((area, feats), F32)
        for ky in range(3):
            total += dot_nn(win_p[pl.ds(y + ky, step)].reshape(area, 3 * feats), rows_ref[0, ky])
        total = total * masked(y)
        for t in range(2):
            rows = total[t * side * breadth : (t + 1) * side * breadth]
            placed = dot_nn(tiling_ref[...], rows.astype(BF16)).astype(BF16)
            tiles[pl.ds((i * 2 + t) * tile_cols, tile_cols)] = placed.reshape(tile_cols, side * side, feats)
        lines = total.reshape(step, breadth, feats)
        for k in range(step // 2):
            high, low = split(lines[2 * k] + lines[2 * k + 1])
            low_grad_ref[i * (step // 2) + k] = (dot_nn(halve, high) + dot_nn(halve, low)).astype(BF16)
        return 0

    lax.fori_loop(0, height // step, last, 0)

    def pick(s, _):
        send_ref[s] = tiles[from_ref[s]]
        return 0

    lax.fori_loop(0, send_ref.shape[0], pick, 0, unroll=8)
    windows(1, 0, win_h_ref)


def front(sizes, low, skip, grad, tissue, base, moves, major, tiling, source):
    height, breadth, feats = skip.shape
    tile_rows, tile_cols = tissue.shape
    wide = (height + 2, breadth, 3 * feats)
    area = height // tile_rows
    vmem = pl.BlockSpec(memory_space=pltpu.VMEM)
    return pl.pallas_call(
        functools.partial(front_kernel, sizes),
        out_shape=(
            jax.ShapeDtypeStruct((source.shape[0], area * area, feats), BF16),
            jax.ShapeDtypeStruct(low.shape, BF16),
            jax.ShapeDtypeStruct(wide, BF16),
            jax.ShapeDtypeStruct(wide, BF16),
            jax.ShapeDtypeStruct(skip.shape, BF16),
            jax.ShapeDtypeStruct(skip.shape, BF16),
            jax.ShapeDtypeStruct((2, 3, feats, 3 * feats), BF16),
            jax.ShapeDtypeStruct((tile_rows, breadth, feats), F32),
        ),
        in_specs=[vmem] * 8 + [pl.BlockSpec(memory_space=pltpu.SMEM)],
        out_specs=(vmem,) * 8,
        scratch_shapes=[
            pltpu.VMEM((2, 2, height, breadth, feats), BF16),
            pltpu.VMEM((2, 2, height, feats), F32),
            pltpu.VMEM((2, 2, 2, height, feats), BF16),
            pltpu.VMEM((2, 2, 2, breadth, feats), BF16),
            pltpu.VMEM((2, 2, 2, height, feats), BF16),
            pltpu.VMEM((2, 4, 2, 16, feats), BF16),
            pltpu.VMEM(wide, BF16),
            pltpu.VMEM(wide, BF16),
            pltpu.VMEM((18, feats, feats), BF16),
            pltpu.VMEM((2, 3, 3 * feats, feats), BF16),
            pltpu.VMEM((tile_rows * tile_cols, area * area, feats), BF16),
            pltpu.VMEM((2, height, feats), F32),
            pltpu.SemaphoreType.DMA((2, 8)),
            pltpu.SemaphoreType.DMA((2, 8)),
        ],
        compiler_params=pltpu.CompilerParams(
            collective_id=0, has_side_effects=True, vmem_limit_bytes=VMEM_BYTES
        ),
        name="front",
    )(low, skip, grad, tissue, base, moves, major, tiling, source)


def back_kernel(
    win_m_ref, win_h_ref, two_ref, pre_ref, lanes_ref, mask_ref, moves_ref, major_ref,
    out_ref, fold_ref, total, lined,
):
    height, breadth, feats = two_ref.shape
    side = height // mask_ref.shape[0]
    chans = feats // G
    step = 2 * side
    area = step * breadth

    total[...] = jnp.zeros_like(total)

    def body(i, _):
        y = i * step
        turned_pre = dot_nt(major_ref[...], pre_ref[pl.ds(y, step)].reshape(area, feats)).astype(BF16)
        turned_two = dot_nt(major_ref[...], two_ref[pl.ds(y, step)].reshape(area, feats)).astype(BF16)
        acc = jnp.zeros((area, feats), F32)
        for ky in range(3):
            merged = win_m_ref[pl.ds(y + ky, step)].reshape(area, 3 * feats)
            hidden = win_h_ref[pl.ds(y + ky, step)].reshape(area, 3 * feats)
            total[0, ky] += dot_nn(turned_pre, merged)
            total[1, ky] += dot_nn(turned_two, hidden)
            acc += dot_nt(hidden, lanes_ref[1, ky])
        two_rows = mask_ref[pl.ds(y // side, 2)]
        mask = jnp.broadcast_to(two_rows[:, None], (2, side, breadth, feats)).reshape(area, feats)
        out_ref[pl.ds(y, step)] = (acc * mask).astype(BF16).reshape(step, breadth, feats)
        return 0

    lax.fori_loop(0, height // step, body, 0)

    fold_ref[...] = jnp.zeros_like(fold_ref)
    for g in range(G):
        for f in range(2):
            for cell in range(9):
                at = (f * 9 + cell_source(g, cell)) * chans
                ky, kx = cell // 3, cell % 3
                lined[at : at + chans, :] = total[
                    f, ky, g * chans : (g + 1) * chans, kx * feats : (kx + 1) * feats
                ]
        high, low = split(lined[...])
        fold_ref[...] += dot_nn(high, moves_ref[g]) + dot_nn(low, moves_ref[g])


def back(win_m, win_h, two, pre, lanes, mask, moves, major):
    feats = two.shape[2]
    vmem = pl.BlockSpec(memory_space=pltpu.VMEM)
    return pl.pallas_call(
        back_kernel,
        out_shape=(
            jax.ShapeDtypeStruct(two.shape, BF16),
            jax.ShapeDtypeStruct((18 * feats // G, feats), F32),
        ),
        in_specs=[vmem] * 8,
        out_specs=(vmem, vmem),
        scratch_shapes=[
            pltpu.VMEM((2, 3, feats, 3 * feats), F32),
            pltpu.VMEM((18 * feats // G, feats), F32),
        ],
        compiler_params=pltpu.CompilerParams(vmem_limit_bytes=VMEM_BYTES),
        cost_estimate=pl.CostEstimate(flops=8 * 10**9, bytes_accessed=12 * 10**6, transcendentals=0),
        name="back",
    )(win_m, win_h, two, pre, lanes, mask, moves, major)


def place_kernel(at_ref, got_ref, out_ref):
    def put(s, _):
        out_ref[s] = got_ref[at_ref[s]]
        return 0

    lax.fori_loop(0, out_ref.shape[0], put, 0, unroll=8)


def place(at, got):
    vmem = pl.BlockSpec(memory_space=pltpu.VMEM)
    return pl.pallas_call(
        place_kernel,
        out_shape=jax.ShapeDtypeStruct((at.shape[0],) + got.shape[1:], BF16),
        in_specs=[pl.BlockSpec(memory_space=pltpu.SMEM), vmem],
        out_specs=vmem,
        compiler_params=pltpu.CompilerParams(vmem_limit_bytes=VMEM_BYTES),
        name="place",
    )(at, got)


def on_device(sizes, low_feats, skip_feats, tissue_mask, owner_slot, filter_one, filter_two, out_grad):
    axes = ("rows", "cols")
    count = sizes[0] * sizes[1]
    height, breadth, feats = skip_feats.shape
    tile_rows, tile_cols = tissue_mask.shape
    tile_count = tile_rows * tile_cols
    side = height // tile_rows
    chans = feats // G
    per_owner = 2 * tile_count // count

    moves = jnp.asarray(feature_moves(feats), BF16)
    major = jnp.asarray(element_major(feats), BF16)
    tiling = jnp.asarray(tile_order(side, breadth), BF16)
    base = jnp.stack([filter_one, filter_two]).reshape(2, chans, 9, feats)
    base = base.transpose(0, 2, 1, 3).reshape(18 * chans, feats)

    slot_list = owner_slot.reshape(-1)
    owner, local = slot_list // tile_count, slot_list % tile_count
    before = (owner[:, None] == owner[None, :]) & (local[None, :] < local[:, None])
    position = owner * per_owner + jnp.sum(before.astype(jnp.int32), axis=1)
    picked = position[None, :] == jnp.arange(count * per_owner, dtype=jnp.int32)[:, None]
    numbers = jnp.arange(tile_count, dtype=jnp.int32)
    source = jnp.sum(jnp.where(picked, numbers[None, :], 0), axis=1).astype(jnp.int32)
    send_slots = jnp.sum(jnp.where(picked, local[None, :] + 1, 0), axis=1).astype(jnp.int32)

    send, low_grad, win_m, win_h, two, pre, lanes, mask = front(
        sizes, low_feats, skip_feats, out_grad, tissue_mask, base, moves, major, tiling, source
    )
    got = lax.all_to_all(send, axes, split_axis=0, concat_axis=0, tiled=True)
    output, folded = back(win_m, win_h, two, pre, lanes, mask, moves, major)

    lines = folded.shape[0]
    share = -(-lines // count)
    terms = jnp.pad(folded, ((0, count * share - lines), (0, 0))).astype(BF16).reshape(count, share, feats)
    slots = jnp.pad(send_slots.astype(BF16).reshape(count, 1, per_owner), ((0, 0), (0, 0), (0, feats - per_owner)))
    packet = jnp.concatenate([terms, slots], axis=1)
    packet = jnp.pad(packet, ((0, 0), (0, -(share + 1) % 16), (0, 0)))
    arrived = lax.all_to_all(packet, axes, split_axis=0, concat_axis=0, tiled=True).astype(F32)
    scale = 1.0 / math.sqrt(height * breadth * count)
    summed = jnp.sum(arrived[:, :share], axis=0) * scale
    whole = lax.all_to_all(
        jnp.broadcast_to(summed[None], (count, share, feats)), axes, split_axis=0, concat_axis=0, tiled=True
    )
    grads = whole.reshape(count * share, feats)[:lines].reshape(2, 9, chans, feats)
    grads = grads.transpose(0, 2, 1, 3).reshape(2, chans, 3, 3, feats)

    got_slots = arrived[:, share, :per_owner].reshape(-1).astype(jnp.int32) - 1
    match = got_slots[None, :] == numbers[:, None]
    at = jnp.sum(jnp.where(match, jnp.arange(count * per_owner, dtype=jnp.int32)[None, :], 0), axis=1)
    skip_grad = place(at.astype(jnp.int32), got).reshape(tile_count, side, side, feats)
    return output, skip_grad, low_grad, grads[0], grads[1]


def solution(mesh):
    sizes = (mesh.shape["rows"], mesh.shape["cols"])
    block = P("rows", "cols", None)
    return jax.shard_map(
        functools.partial(on_device, sizes),
        mesh=mesh,
        in_specs=(block, block, P("rows", "cols"), P("rows", "cols"), P(), P(), block),
        out_specs=(block, P(("rows", "cols"), None, None, None), block, P(), P()),
        check_vma=False,
    )
```

```python
import functools
import math

import jax
import jax.numpy as jnp
import numpy as np
from jax import lax
from jax.experimental import pallas as pl
from jax.experimental.pallas import tpu as pltpu
from jax.sharding import PartitionSpec as P

G = 8
MESH = pl.DeviceIdType.MESH
F32 = jnp.float32
BF16 = jnp.bfloat16
VMEM_BYTES = 56 * 1024 * 1024


def element_inverse(element):
    mirror, turns = element // 4, element % 4
    return element if mirror else (4 - turns) % 4


def element_product(first, second):
    mirror = (first // 4 + second // 4) % 2
    turns = (first % 4 + (1 - 2 * (first // 4)) * (second % 4)) % 4
    return mirror * 4 + turns


def element_act(element, row_off, col_off):
    mirror, turns = element // 4, element % 4
    row_now, col_now = row_off, -col_off if mirror else col_off
    for _ in range(turns):
        row_now, col_now = -col_now, row_now
    return row_now, col_now


def cell_source(element, cell):
    row, col = element_act(element_inverse(element), cell // 3 - 1, cell % 3 - 1)
    return (row + 1) * 3 + col + 1


def feature_moves(features):
    moves = np.zeros((G, features, features), np.float32)
    for elem in range(G):
        for i in range(features):
            moves[elem, i, i // G * G + element_product(element_inverse(elem), i % G)] = 1
    return moves


def element_major(features):
    channels = features // G
    order = np.zeros((features, features), np.float32)
    for o in range(channels):
        for g in range(G):
            order[g * channels + o, o * G + g] = 1
    return order


def tile_order(side, breadth):
    order = np.zeros((side * breadth, side * breadth), np.float32)
    for py in range(side):
        for x in range(breadth):
            order[(x // side * side + py) * side + x % side, py * breadth + x] = 1
    return order


def dot_nn(a, b):
    return lax.dot_general(a, b, (((1,), (0,)), ((), ())), preferred_element_type=F32)


def dot_nt(a, b):
    return lax.dot_general(a, b, (((1,), (1,)), ((), ())), preferred_element_type=F32)


def split(value):
    high = value.astype(BF16)
    return high, (value - high.astype(F32)).astype(BF16)


def shifted(row, left, right):
    breadth = row.shape[0]
    at = lax.broadcasted_iota(jnp.int32, row.shape, 0)
    before = jnp.where(at == 0, left, pltpu.roll(row, 1, 0))
    after = jnp.where(at == breadth - 1, right, pltpu.roll(row, breadth - 1, 0))
    return before.astype(BF16), after.astype(BF16)


def whole_kernel(
    shape,
    low_ref, skip_ref, grad_ref, tissue_ref, base_ref, moves_ref, major_ref, tiling_ref, slots_ref, from_ref,
    out_ref, low_grad_ref, got_ref, got_slots_ref, sums_ref,
    send_ref, win_m_ref, win_h_ref, two_ref, pre_ref, lanes_ref, mask_ref,
    field, ends, wire, got_row, got_col, got_cor, win_g, win_p, gathered, rows_ref, tiles, halo32,
    total, lined, folded, quarter_out, quarter_in, quarter_sum, part_out, part_in, part_sum, part_all,
    near, send_sem, recv_sem, tile_sem, slot_sem, fold_sems,
):
    nr, nc = shape
    count = nr * nc
    height, breadth, feats = skip_ref.shape
    tile_rows, tile_cols = tissue_ref.shape
    side = height // tile_rows
    chans = feats // G
    r, c = lax.axis_index("rows"), lax.axis_index("cols")
    me = r * nc + c
    up, down = lax.rem(r + nr - 1, nr), lax.rem(r + 1, nr)
    west, east = lax.rem(c + nc - 1, nc), lax.rem(c + 1, nc)
    around = ((up, c), (down, c), (r, west), (r, east), (up, west), (up, east), (down, west), (down, east))

    def ahead(i, j):
        return lax.rem(r + i, nr), lax.rem(c + j, nc)

    offsets = sorted(
        ((i, j) for i in range(nr) for j in range(nc) if i or j), key=lambda ij: (abs(2 * ij[1] - nc), ij)
    )

    barrier = pltpu.get_barrier_semaphore()
    for i, j in offsets:
        pl.semaphore_signal(barrier, inc=1, device_id=ahead(i, j), device_id_type=MESH)

    spread = (
        lax.broadcasted_iota(jnp.int32, (breadth, tile_cols), 0) // side
        == lax.broadcasted_iota(jnp.int32, (breadth, tile_cols), 1)
    )
    ones = jnp.ones((tile_cols, feats), BF16)
    for tr in range(tile_rows):
        held = jnp.where(spread, tissue_ref[tr : tr + 1, :].astype(F32), 0.0).astype(BF16)
        mask_ref[tr] = dot_nn(held, ones)

    double = (
        lax.broadcasted_iota(jnp.int32, (breadth, breadth // 2), 0) // 2
        == lax.broadcasted_iota(jnp.int32, (breadth, breadth // 2), 1)
    ).astype(F32).astype(BF16)

    def enter(pair, _):
        raised = dot_nn(double, low_ref[pair])
        mask = mask_ref[pair * 2 // side]
        for k in range(2):
            y = pair * 2 + k
            merged = (raised + skip_ref[y].astype(F32)) * mask
            two = grad_ref[y].astype(F32) * mask
            field[0, 0, y] = merged.astype(BF16)
            field[0, 1, y] = two.astype(BF16)
            two_ref[y] = two.astype(BF16)
            for f, value in enumerate((merged, two)):
                ends[0, f, pl.ds(y, 1), :] = value[0:1]
                ends[1, f, pl.ds(y, 1), :] = value[breadth - 1 : breadth]
        return 0

    lax.fori_loop(0, height // 2, enter, 0)

    def copies(ph):
        low_end, high_end = pl.ds(0, 16), pl.ds(breadth - 16, 16)
        plan = (
            (field.at[ph, :, 0], got_row.at[ph, 1]),
            (field.at[ph, :, height - 1], got_row.at[ph, 0]),
            (wire.at[ph, 0], got_col.at[ph, 1]),
            (wire.at[ph, 1], got_col.at[ph, 0]),
            (field.at[ph, :, 0, low_end], got_cor.at[ph, 3]),
            (field.at[ph, :, 0, high_end], got_cor.at[ph, 2]),
            (field.at[ph, :, height - 1, low_end], got_cor.at[ph, 1]),
            (field.at[ph, :, height - 1, high_end], got_cor.at[ph, 0]),
        )
        return [
            pltpu.make_async_remote_copy(
                src_ref=src, dst_ref=dst, send_sem=send_sem.at[ph, k], recv_sem=recv_sem.at[ph, k],
                device_id=around[k], device_id_type=MESH,
            )
            for k, (src, dst) in enumerate(plan)
        ]

    def send_halo(ph):
        wire[ph] = ends[...].astype(BF16)
        started = copies(ph)
        for copy in started:
            copy.start()
        return started

    in_up = jnp.where(r > 0, 1.0, 0.0)
    in_down = jnp.where(r < nr - 1, 1.0, 0.0)
    in_west = jnp.where(c > 0, 1.0, 0.0)
    in_east = jnp.where(c < nc - 1, 1.0, 0.0)

    def windows(ph, f, out):
        halo32[0] = got_col[ph, 0, f].astype(F32) * in_west
        halo32[1] = got_col[ph, 1, f].astype(F32) * in_east

        def put(y, row, left, right):
            before, after = shifted(row, left, right)
            out[y, :, 0:feats] = before
            out[y, :, feats : 2 * feats] = row.astype(BF16)
            out[y, :, 2 * feats : 3 * feats] = after

        def inner(y, _):
            put(y + 1, field[ph, f, y].astype(F32), halo32[0, pl.ds(y, 1), :], halo32[1, pl.ds(y, 1), :])
            return 0

        lax.fori_loop(0, height, inner, 0)
        for k, (y, gate) in enumerate(((0, in_up), (height + 1, in_down))):
            row = got_row[ph, k, f].astype(F32) * gate
            left = got_cor[ph, 2 * k, f].astype(F32)[15:16] * (gate * in_west)
            right = got_cor[ph, 2 * k + 1, f].astype(F32)[0:1] * (gate * in_east)
            put(y, row, left, right)

    pl.semaphore_wait(barrier, count - 1)
    first = send_halo(0)

    def push(src, dst, sems, k, device):
        copy = pltpu.make_async_remote_copy(
            src_ref=src, dst_ref=dst, send_sem=sems.at[0, k], recv_sem=sems.at[1, k],
            device_id=device, device_id_type=MESH,
        )
        copy.start()
        return copy

    late = []
    for k, (i, j) in enumerate(offsets):
        to = ahead(i, j)
        late.append(push(slots_ref.at[to[0] * nc + to[1]], got_slots_ref.at[me], slot_sem, k, to))
    got_slots_ref[me] = slots_ref[me]

    def gather(g):
        placed = dot_nt(base_ref[...], moves_ref[g]).astype(BF16)
        for f in range(2):
            for cell in range(9):
                at = (f * 9 + cell_source(g, cell)) * chans
                gathered[f * 9 + cell, g * chans : (g + 1) * chans, :] = placed[at : at + chans]

    for g in range(G):
        gather(g)
    for f in range(2):
        for ky in range(3):
            for kx in range(3):
                full = lax.dot_general(
                    major_ref[...], gathered[f * 9 + ky * 3 + kx], (((0,), (0,)), ((), ())),
                    preferred_element_type=F32,
                ).astype(BF16)
                lanes_ref[f, ky, :, kx * feats : (kx + 1) * feats] = full
                rows_ref[f, 2 - ky, (2 - kx) * feats : (3 - kx) * feats, :] = full

    for copy in first:
        copy.wait()
    windows(0, 0, win_m_ref)
    windows(0, 1, win_g)

    step = 2 * side
    area = step * breadth

    def masked(y):
        two_rows = mask_ref[pl.ds(y // side, 2)]
        return jnp.broadcast_to(two_rows[:, None], (2, side, breadth, feats)).reshape(area, feats)

    def middle(i, _):
        y = i * step
        pre = jnp.zeros((area, feats), F32)
        back = jnp.zeros((area, feats), F32)
        for ky in range(3):
            pre += dot_nt(win_m_ref[pl.ds(y + ky, step)].reshape(area, 3 * feats), lanes_ref[0, ky])
            back += dot_nn(win_g[pl.ds(y + ky, step)].reshape(area, 3 * feats), rows_ref[1, ky])
        mask = masked(y)
        sigma = jax.nn.sigmoid(pre)
        hidden = (pre * sigma * mask).reshape(step, breadth, feats)
        slope = (back * (sigma * (1.0 + pre * (1.0 - sigma))) * mask).reshape(step, breadth, feats)
        for f, value in enumerate((hidden, slope)):
            field[1, f, pl.ds(y, step)] = value.astype(BF16)
            for k in range(step):
                ends[0, f, pl.ds(y + k, 1), :] = value[k, 0:1]
                ends[1, f, pl.ds(y + k, 1), :] = value[k, breadth - 1 : breadth]
        pre_ref[pl.ds(y, step)] = slope.astype(BF16)
        return 0

    lax.fori_loop(0, height // step, middle, 0)
    second = send_halo(1)
    for copy in second:
        copy.wait()
    windows(1, 1, win_p)

    halve = (
        lax.broadcasted_iota(jnp.int32, (breadth // 2, breadth), 1) // 2
        == lax.broadcasted_iota(jnp.int32, (breadth // 2, breadth), 0)
    ).astype(F32).astype(BF16)

    def last(i, _):
        y = i * step
        total = jnp.zeros((area, feats), F32)
        for ky in range(3):
            total += dot_nn(win_p[pl.ds(y + ky, step)].reshape(area, 3 * feats), rows_ref[0, ky])
        total = total * masked(y)
        for t in range(2):
            rows = total[t * side * breadth : (t + 1) * side * breadth]
            placed = dot_nn(tiling_ref[...], rows.astype(BF16)).astype(BF16)
            tiles[pl.ds((i * 2 + t) * tile_cols, tile_cols)] = placed.reshape(tile_cols, side * side, feats)
        lines = total.reshape(step, breadth, feats)
        for k in range(step // 2):
            high, low = split(lines[2 * k] + lines[2 * k + 1])
            low_grad_ref[i * (step // 2) + k] = (dot_nn(halve, high) + dot_nn(halve, low)).astype(BF16)
        return 0

    lax.fori_loop(0, height // step, last, 0)

    def pick(s, _):
        send_ref[s] = tiles[from_ref[s]]
        return 0

    lax.fori_loop(0, send_ref.shape[0], pick, 0, unroll=8)

    each = send_ref.shape[0] // count
    for k, (i, j) in enumerate(offsets):
        to = ahead(i, j)
        late.append(push(
            send_ref.at[pl.ds((to[0] * nc + to[1]) * each, each)], got_ref.at[pl.ds(me * each, each)],
            tile_sem, k, to,
        ))
    got_ref[pl.ds(me * each, each)] = send_ref[pl.ds(me * each, each)]

    windows(1, 0, win_h_ref)
    total[...] = jnp.zeros_like(total)

    def terms(i, _):
        y = i * step
        turned_pre = dot_nt(major_ref[...], pre_ref[pl.ds(y, step)].reshape(area, feats)).astype(BF16)
        turned_two = dot_nt(major_ref[...], two_ref[pl.ds(y, step)].reshape(area, feats)).astype(BF16)
        for ky in range(3):
            merged = win_m_ref[pl.ds(y + ky, step)].reshape(area, 3 * feats)
            hidden = win_h_ref[pl.ds(y + ky, step)].reshape(area, 3 * feats)
            total[0, ky] += dot_nn(turned_pre, merged)
            total[1, ky] += dot_nn(turned_two, hidden)
        return 0

    lax.fori_loop(0, height // step, terms, 0)

    folded[...] = jnp.zeros_like(folded)
    lines = 18 * chans
    for g in range(G):
        for f in range(2):
            for cell in range(9):
                at = (f * 9 + cell_source(g, cell)) * chans
                ky, kx = cell // 3, cell % 3
                lined[at : at + chans, :] = total[
                    f, ky, g * chans : (g + 1) * chans, kx * feats : (kx + 1) * feats
                ]
        high, low = split(lined[...])
        folded[:lines] += dot_nn(high, moves_ref[g]) + dot_nn(low, moves_ref[g])

    quarter, part = quarter_sum.shape[0], quarter_sum.shape[0] // nc
    quarter_out[...] = folded[...].astype(BF16).reshape(nr, quarter, feats)
    wave = []
    for i in range(1, nr):
        to = ahead(i, 0)
        wave.append(push(quarter_out.at[to[0]], quarter_in.at[i - 1], fold_sems.at[0], i, to))

    def outer(i, _):
        y = i * step
        acc = jnp.zeros((area, feats), F32)
        for ky in range(3):
            acc += dot_nt(win_h_ref[pl.ds(y + ky, step)].reshape(area, 3 * feats), lanes_ref[1, ky])
        out_ref[pl.ds(y, step)] = (acc * masked(y)).astype(BF16).reshape(step, breadth, feats)
        return 0

    lax.fori_loop(0, height // step, outer, 0)

    for copy in wave:
        copy.wait()
    summed = quarter_out[r].astype(F32)
    for i in range(1, nr):
        summed += quarter_in[i - 1].astype(F32)
    quarter_sum[...] = summed
    for j in range(nc):
        part_out[j, :part] = quarter_sum[j * part : (j + 1) * part]
    wave = []
    for j in range(1, nc):
        to = ahead(0, j)
        wave.append(push(part_out.at[to[1]], part_in.at[j - 1], fold_sems.at[1], j, to))
    for copy in wave:
        copy.wait()
    share = part_out[c]
    for j in range(1, nc):
        share += part_in[j - 1]
    part_sum[...] = share
    part_all[c] = share
    wave = []
    for j in range(1, nc):
        wave.append(push(part_sum, part_all.at[c], fold_sems.at[2], j, ahead(0, j)))
    for copy in wave:
        copy.wait()
    for j in range(nc):
        quarter_sum[j * part : (j + 1) * part] = part_all[j, :part]
    rounded = quarter_sum[...].astype(BF16)
    near[...] = rounded
    sums_ref[r] = rounded
    wave = []
    for i in range(1, nr):
        wave.append(push(near, sums_ref.at[r], fold_sems.at[3], i, ahead(i, 0)))
    for copy in wave:
        copy.wait()
    for copy in late:
        copy.wait()


def whole(sizes, low, skip, grad, tissue, base, moves, major, tiling, slots, source):
    nr, nc = sizes
    height, breadth, feats = skip.shape
    tile_rows, tile_cols = tissue.shape
    wide = (height + 2, breadth, 3 * feats)
    side = height // tile_rows
    blocks = (source.shape[0], side * side, feats)
    lines = 18 * feats // G
    unit = nc * 16 // math.gcd(nc, 16)
    quarter = -(-lines // (nr * unit)) * unit
    part = quarter // nc
    padded = -(-part // 8) * 8
    vmem = pl.BlockSpec(memory_space=pltpu.VMEM)
    return pl.pallas_call(
        functools.partial(whole_kernel, sizes),
        out_shape=(
            jax.ShapeDtypeStruct(skip.shape, BF16),
            jax.ShapeDtypeStruct(low.shape, BF16),
            jax.ShapeDtypeStruct(blocks, BF16),
            jax.ShapeDtypeStruct(slots.shape, F32),
            jax.ShapeDtypeStruct((nr, quarter, feats), BF16),
        ),
        in_specs=[vmem] * 9 + [pl.BlockSpec(memory_space=pltpu.SMEM)],
        out_specs=(vmem,) * 5,
        scratch_shapes=[
            pltpu.VMEM(blocks, BF16),
            pltpu.VMEM(wide, BF16),
            pltpu.VMEM(wide, BF16),
            pltpu.VMEM(skip.shape, BF16),
            pltpu.VMEM(skip.shape, BF16),
            pltpu.VMEM((2, 3, feats, 3 * feats), BF16),
            pltpu.VMEM((tile_rows, breadth, feats), F32),
            pltpu.VMEM((2, 2, height, breadth, feats), BF16),
            pltpu.VMEM((2, 2, height, feats), F32),
            pltpu.VMEM((2, 2, 2, height, feats), BF16),
            pltpu.VMEM((2, 2, 2, breadth, feats), BF16),
            pltpu.VMEM((2, 2, 2, height, feats), BF16),
            pltpu.VMEM((2, 4, 2, 16, feats), BF16),
            pltpu.VMEM(wide, BF16),
            pltpu.VMEM(wide, BF16),
            pltpu.VMEM((18, feats, feats), BF16),
            pltpu.VMEM((2, 3, 3 * feats, feats), BF16),
            pltpu.VMEM((tile_rows * tile_cols, side * side, feats), BF16),
            pltpu.VMEM((2, height, feats), F32),
            pltpu.VMEM((2, 3, feats, 3 * feats), F32),
            pltpu.VMEM((lines, feats), F32),
            pltpu.VMEM((nr * quarter, feats), F32),
            pltpu.VMEM((nr, quarter, feats), BF16),
            pltpu.VMEM((nr - 1, quarter, feats), BF16),
            pltpu.VMEM((quarter, feats), F32),
            pltpu.VMEM((nc, padded, feats), F32),
            pltpu.VMEM((nc - 1, padded, feats), F32),
            pltpu.VMEM((padded, feats), F32),
            pltpu.VMEM((nc, padded, feats), F32),
            pltpu.VMEM((quarter, feats), BF16),
            pltpu.SemaphoreType.DMA((2, 8)),
            pltpu.SemaphoreType.DMA((2, 8)),
            pltpu.SemaphoreType.DMA((2, nr * nc)),
            pltpu.SemaphoreType.DMA((2, nr * nc)),
            pltpu.SemaphoreType.DMA((4, 2, max(nr, nc))),
        ],
        compiler_params=pltpu.CompilerParams(
            collective_id=0, has_side_effects=True, vmem_limit_bytes=VMEM_BYTES
        ),
        name="whole",
    )(low, skip, grad, tissue, base, moves, major, tiling, slots, source)


def place_kernel(at_ref, got_ref, out_ref):
    def put(s, _):
        out_ref[s] = got_ref[at_ref[s]]
        return 0

    lax.fori_loop(0, out_ref.shape[0], put, 0, unroll=8)


def place(at, got):
    vmem = pl.BlockSpec(memory_space=pltpu.VMEM)
    return pl.pallas_call(
        place_kernel,
        out_shape=jax.ShapeDtypeStruct((at.shape[0],) + got.shape[1:], BF16),
        in_specs=[pl.BlockSpec(memory_space=pltpu.SMEM), vmem],
        out_specs=vmem,
        compiler_params=pltpu.CompilerParams(vmem_limit_bytes=VMEM_BYTES),
        name="place",
    )(at, got)


def on_device(sizes, low_feats, skip_feats, tissue_mask, owner_slot, filter_one, filter_two, out_grad):
    count = sizes[0] * sizes[1]
    height, breadth, feats = skip_feats.shape
    tile_rows, tile_cols = tissue_mask.shape
    tile_count = tile_rows * tile_cols
    side = height // tile_rows
    chans = feats // G
    per_owner = 2 * tile_count // count

    moves = jnp.asarray(feature_moves(feats), BF16)
    major = jnp.asarray(element_major(feats), BF16)
    tiling = jnp.asarray(tile_order(side, breadth), BF16)
    base = jnp.stack([filter_one, filter_two]).reshape(2, chans, 9, feats)
    base = base.transpose(0, 2, 1, 3).reshape(18 * chans, feats)

    slot_list = owner_slot.reshape(-1)
    owner, local = slot_list // tile_count, slot_list % tile_count
    before = (owner[:, None] == owner[None, :]) & (local[None, :] < local[:, None])
    position = owner * per_owner + jnp.sum(before.astype(jnp.int32), axis=1)
    picked = position[None, :] == jnp.arange(count * per_owner, dtype=jnp.int32)[:, None]
    numbers = jnp.arange(tile_count, dtype=jnp.int32)
    source = jnp.sum(jnp.where(picked, numbers[None, :], 0), axis=1).astype(jnp.int32)
    send_slots = jnp.sum(jnp.where(picked, local[None, :] + 1, 0), axis=1).astype(jnp.int32)

    slots = jnp.broadcast_to(send_slots.astype(F32).reshape(count, per_owner, 1), (count, per_owner, 128))
    slots = jnp.pad(slots, ((0, 0), (0, -per_owner % 8), (0, 0)))
    output, low_grad, got, got_slots, sums = whole(
        sizes, low_feats, skip_feats, out_grad, tissue_mask, base, moves, major, tiling, slots, source
    )
    scale = 1.0 / math.sqrt(height * breadth * count)
    lines = 18 * chans
    grads = sums.astype(F32).reshape(-1, feats)[:lines].reshape(2, 9, chans, feats) * scale
    grads = grads.transpose(0, 2, 1, 3).reshape(2, chans, 3, 3, feats)

    got_slots = got_slots[:, :per_owner, 0].reshape(-1).astype(jnp.int32) - 1
    match = got_slots[None, :] == numbers[:, None]
    at = jnp.sum(jnp.where(match, jnp.arange(count * per_owner, dtype=jnp.int32)[None, :], 0), axis=1)
    skip_grad = place(at.astype(jnp.int32), got).reshape(tile_count, side, side, feats)
    return output, skip_grad, low_grad, grads[0], grads[1]


def solution(mesh):
    sizes = (mesh.shape["rows"], mesh.shape["cols"])
    block = P("rows", "cols", None)
    return jax.shard_map(
        functools.partial(on_device, sizes),
        mesh=mesh,
        in_specs=(block, block, P("rows", "cols"), P("rows", "cols"), P(), P(), block),
        out_specs=(block, P(("rows", "cols"), None, None, None), block, P(), P()),
        check_vma=False,
    )
```

```python
import functools
import math

import jax
import jax.numpy as jnp
import numpy as np
from jax import lax
from jax.experimental import pallas as pl
from jax.experimental.pallas import tpu as pltpu
from jax.sharding import PartitionSpec as P

G = 8
MESH = pl.DeviceIdType.MESH
F32 = jnp.float32
BF16 = jnp.bfloat16
VMEM_BYTES = 56 * 1024 * 1024


def element_inverse(element):
    mirror, turns = element // 4, element % 4
    return element if mirror else (4 - turns) % 4


def element_product(first, second):
    mirror = (first // 4 + second // 4) % 2
    turns = (first % 4 + (1 - 2 * (first // 4)) * (second % 4)) % 4
    return mirror * 4 + turns


def element_act(element, row_off, col_off):
    mirror, turns = element // 4, element % 4
    row_now, col_now = row_off, -col_off if mirror else col_off
    for _ in range(turns):
        row_now, col_now = -col_now, row_now
    return row_now, col_now


def cell_source(element, cell):
    row, col = element_act(element_inverse(element), cell // 3 - 1, cell % 3 - 1)
    return (row + 1) * 3 + col + 1


def feature_moves(features):
    moves = np.zeros((G, features, features), np.float32)
    for elem in range(G):
        for i in range(features):
            moves[elem, i, i // G * G + element_product(element_inverse(elem), i % G)] = 1
    return moves


def element_major(features):
    channels = features // G
    order = np.zeros((features, features), np.float32)
    for o in range(channels):
        for g in range(G):
            order[g * channels + o, o * G + g] = 1
    return order


def tile_order(side, breadth):
    order = np.zeros((side * breadth, side * breadth), np.float32)
    for py in range(side):
        for x in range(breadth):
            order[(x // side * side + py) * side + x % side, py * breadth + x] = 1
    return order


def dot_nn(a, b):
    return lax.dot_general(a, b, (((1,), (0,)), ((), ())), preferred_element_type=F32)


def dot_nt(a, b):
    return lax.dot_general(a, b, (((1,), (1,)), ((), ())), preferred_element_type=F32)


def split(value):
    high = value.astype(BF16)
    return high, (value - high.astype(F32)).astype(BF16)


def shifted(row, left, right):
    breadth = row.shape[0]
    at = lax.broadcasted_iota(jnp.int32, row.shape, 0)
    before = jnp.where(at == 0, left, pltpu.roll(row, 1, 0))
    after = jnp.where(at == breadth - 1, right, pltpu.roll(row, breadth - 1, 0))
    return before.astype(BF16), after.astype(BF16)


def whole_kernel(
    shape,
    low_ref, skip_ref, grad_ref, tissue_ref, base_ref, moves_ref, major_ref, tiling_ref, slots_ref, from_ref,
    out_ref, low_grad_ref, got_ref, got_slots_ref, sums_ref,
    send_ref, win_m_ref, win_h_ref, two_ref, pre_ref, lanes_ref, mask_ref,
    field, ends, wire, got_row, got_col, got_cor, win_g, win_p, gathered, rows_ref, tiles, halo32,
    total, lined, folded, quarter_out, quarter_in, quarter_sum, part_out, part_in, part_sum, part_all,
    near, kept, send_sem, recv_sem, tile_sem, slot_sem, fold_sems,
):
    nr, nc = shape
    count = nr * nc
    height, breadth, feats = skip_ref.shape
    tile_rows, tile_cols = tissue_ref.shape
    side = height // tile_rows
    chans = feats // G
    r, c = lax.axis_index("rows"), lax.axis_index("cols")
    me = r * nc + c
    up, down = lax.rem(r + nr - 1, nr), lax.rem(r + 1, nr)
    west, east = lax.rem(c + nc - 1, nc), lax.rem(c + 1, nc)
    around = ((up, c), (down, c), (r, west), (r, east), (up, west), (up, east), (down, west), (down, east))

    def ahead(i, j):
        return lax.rem(r + i, nr), lax.rem(c + j, nc)

    offsets = sorted(
        ((i, j) for i in range(nr) for j in range(nc) if i or j), key=lambda ij: (abs(2 * ij[1] - nc), ij)
    )

    barrier = pltpu.get_barrier_semaphore()
    for i, j in offsets:
        pl.semaphore_signal(barrier, inc=1, device_id=ahead(i, j), device_id_type=MESH)

    spread = (
        lax.broadcasted_iota(jnp.int32, (breadth, tile_cols), 0) // side
        == lax.broadcasted_iota(jnp.int32, (breadth, tile_cols), 1)
    )
    ones = jnp.ones((tile_cols, feats), BF16)
    for tr in range(tile_rows):
        held = jnp.where(spread, tissue_ref[tr : tr + 1, :].astype(F32), 0.0).astype(BF16)
        mask_ref[tr] = dot_nn(held, ones)

    double = (
        lax.broadcasted_iota(jnp.int32, (breadth, breadth // 2), 0) // 2
        == lax.broadcasted_iota(jnp.int32, (breadth, breadth // 2), 1)
    ).astype(F32).astype(BF16)

    def enter(pair, _):
        raised = dot_nn(double, low_ref[pair])
        mask = mask_ref[pair * 2 // side]
        for k in range(2):
            y = pair * 2 + k
            merged = (raised + skip_ref[y].astype(F32)) * mask
            two = grad_ref[y].astype(F32) * mask
            field[0, 0, y] = merged.astype(BF16)
            field[0, 1, y] = two.astype(BF16)
            two_ref[y] = two.astype(BF16)
            for f, value in enumerate((merged, two)):
                ends[0, f, pl.ds(y, 1), :] = value[0:1]
                ends[1, f, pl.ds(y, 1), :] = value[breadth - 1 : breadth]
        return 0

    lax.fori_loop(0, height // 2, enter, 0, unroll=2)

    def copies(ph):
        low_end, high_end = pl.ds(0, 16), pl.ds(breadth - 16, 16)
        plan = (
            (field.at[ph, :, 0], got_row.at[ph, 1]),
            (field.at[ph, :, height - 1], got_row.at[ph, 0]),
            (wire.at[ph, 0], got_col.at[ph, 1]),
            (wire.at[ph, 1], got_col.at[ph, 0]),
            (field.at[ph, :, 0, low_end], got_cor.at[ph, 3]),
            (field.at[ph, :, 0, high_end], got_cor.at[ph, 2]),
            (field.at[ph, :, height - 1, low_end], got_cor.at[ph, 1]),
            (field.at[ph, :, height - 1, high_end], got_cor.at[ph, 0]),
        )
        return [
            pltpu.make_async_remote_copy(
                src_ref=src, dst_ref=dst, send_sem=send_sem.at[ph, k], recv_sem=recv_sem.at[ph, k],
                device_id=around[k], device_id_type=MESH,
            )
            for k, (src, dst) in enumerate(plan)
        ]

    def send_halo(ph):
        wire[ph] = ends[...].astype(BF16)
        started = copies(ph)
        for copy in started:
            copy.start()
        return started

    in_up = jnp.where(r > 0, 1.0, 0.0)
    in_down = jnp.where(r < nr - 1, 1.0, 0.0)
    in_west = jnp.where(c > 0, 1.0, 0.0)
    in_east = jnp.where(c < nc - 1, 1.0, 0.0)

    def windows(ph, f, out):
        halo32[0] = got_col[ph, 0, f].astype(F32) * in_west
        halo32[1] = got_col[ph, 1, f].astype(F32) * in_east

        def put(y, row, left, right):
            before, after = shifted(row, left, right)
            out[y, :, 0:feats] = before
            out[y, :, feats : 2 * feats] = row.astype(BF16)
            out[y, :, 2 * feats : 3 * feats] = after

        def inner(y, _):
            put(y + 1, field[ph, f, y].astype(F32), halo32[0, pl.ds(y, 1), :], halo32[1, pl.ds(y, 1), :])
            return 0

        lax.fori_loop(0, height, inner, 0, unroll=4)
        for k, (y, gate) in enumerate(((0, in_up), (height + 1, in_down))):
            row = got_row[ph, k, f].astype(F32) * gate
            left = got_cor[ph, 2 * k, f].astype(F32)[15:16] * (gate * in_west)
            right = got_cor[ph, 2 * k + 1, f].astype(F32)[0:1] * (gate * in_east)
            put(y, row, left, right)

    pl.semaphore_wait(barrier, count - 1)
    first = send_halo(0)

    def push(src, dst, sems, k, device):
        copy = pltpu.make_async_remote_copy(
            src_ref=src, dst_ref=dst, send_sem=sems.at[0, k], recv_sem=sems.at[1, k],
            device_id=device, device_id_type=MESH,
        )
        copy.start()
        return copy

    late = []
    for k, (i, j) in enumerate(offsets):
        to = ahead(i, j)
        late.append(push(slots_ref.at[to[0] * nc + to[1]], got_slots_ref.at[me], slot_sem, k, to))
    got_slots_ref[me] = slots_ref[me]

    def gather(g):
        placed = dot_nt(base_ref[...], moves_ref[g]).astype(BF16)
        for f in range(2):
            for cell in range(9):
                at = (f * 9 + cell_source(g, cell)) * chans
                gathered[f * 9 + cell, g * chans : (g + 1) * chans, :] = placed[at : at + chans]

    for g in range(G):
        gather(g)
    for f in range(2):
        for ky in range(3):
            for kx in range(3):
                full = lax.dot_general(
                    major_ref[...], gathered[f * 9 + ky * 3 + kx], (((0,), (0,)), ((), ())),
                    preferred_element_type=F32,
                ).astype(BF16)
                lanes_ref[f, ky, :, kx * feats : (kx + 1) * feats] = full
                rows_ref[f, 2 - ky, (2 - kx) * feats : (3 - kx) * feats, :] = full

    for copy in first:
        copy.wait()
    windows(0, 0, win_m_ref)
    windows(0, 1, win_g)

    step = 2 * side
    area = step * breadth

    def masked(y):
        two_rows = mask_ref[pl.ds(y // side, 2)]
        return jnp.broadcast_to(two_rows[:, None], (2, side, breadth, feats)).reshape(area, feats)

    def middle(i, _):
        y = i * step
        pre = jnp.zeros((area, feats), F32)
        back = jnp.zeros((area, feats), F32)
        for ky in range(3):
            pre += dot_nt(win_m_ref[pl.ds(y + ky, step)].reshape(area, 3 * feats), lanes_ref[0, ky])
            back += dot_nn(win_g[pl.ds(y + ky, step)].reshape(area, 3 * feats), rows_ref[1, ky])
        mask = masked(y)
        sigma = jax.nn.sigmoid(pre)
        hidden = (pre * sigma * mask).reshape(step, breadth, feats)
        slope = (back * (sigma * (1.0 + pre * (1.0 - sigma))) * mask).reshape(step, breadth, feats)
        for f, value in enumerate((hidden, slope)):
            field[1, f, pl.ds(y, step)] = value.astype(BF16)
            for k in range(step):
                ends[0, f, pl.ds(y + k, 1), :] = value[k, 0:1]
                ends[1, f, pl.ds(y + k, 1), :] = value[k, breadth - 1 : breadth]
        pre_ref[pl.ds(y, step)] = slope.astype(BF16)
        return 0

    lax.fori_loop(0, height // step, middle, 0)
    second = send_halo(1)

    def terms(f, grads, window):
        total[f] = jnp.zeros(total.shape[1:], F32)

        def add(i, _):
            y = i * step
            turned = dot_nt(major_ref[...], grads[pl.ds(y, step)].reshape(area, feats)).astype(BF16)
            for ky in range(3):
                total[f, ky] += dot_nn(turned, window[pl.ds(y + ky, step)].reshape(area, 3 * feats))
            return 0

        lax.fori_loop(0, height // step, add, 0)

    terms(0, pre_ref, win_m_ref)
    for copy in second:
        copy.wait()
    windows(1, 1, win_p)

    halve = (
        lax.broadcasted_iota(jnp.int32, (breadth // 2, breadth), 1) // 2
        == lax.broadcasted_iota(jnp.int32, (breadth // 2, breadth), 0)
    ).astype(F32).astype(BF16)

    def last(i, _):
        y = i * step
        total = jnp.zeros((area, feats), F32)
        for ky in range(3):
            total += dot_nn(win_p[pl.ds(y + ky, step)].reshape(area, 3 * feats), rows_ref[0, ky])
        total = total * masked(y)
        for t in range(2):
            rows = total[t * side * breadth : (t + 1) * side * breadth]
            placed = dot_nn(tiling_ref[...], rows.astype(BF16)).astype(BF16)
            tiles[pl.ds((i * 2 + t) * tile_cols, tile_cols)] = placed.reshape(tile_cols, side * side, feats)
        kept[pl.ds(y, step)] = total.reshape(step, breadth, feats)
        return 0

    lax.fori_loop(0, height // step, last, 0)

    each = send_ref.shape[0] // count

    def pick(to):
        base = (to[0] * nc + to[1]) * each
        for q in range(each):
            send_ref[base + q] = tiles[from_ref[base + q]]
        return pl.ds(base, each)

    queue = list(enumerate(offsets))

    def send_tiles(part_of):
        for _ in range(min(len(queue), len(offsets) * part_of // 32 + 1)):
            k, (i, j) = queue.pop(0)
            to = ahead(i, j)
            blocks = pick(to)
            late.append(push(send_ref.at[blocks], got_ref.at[pl.ds(me * each, each)], tile_sem, k, to))

    send_tiles(9)
    own = pick((r, c))
    got_ref[own] = send_ref[own]

    windows(1, 0, win_h_ref)
    terms(1, two_ref, win_h_ref)

    folded[...] = jnp.zeros_like(folded)
    lines = 18 * chans
    for g in range(G):
        for f in range(2):
            for cell in range(9):
                at = (f * 9 + cell_source(g, cell)) * chans
                ky, kx = cell // 3, cell % 3
                lined[at : at + chans, :] = total[
                    f, ky, g * chans : (g + 1) * chans, kx * feats : (kx + 1) * feats
                ]
        high, low = split(lined[...])
        folded[:lines] += dot_nn(high, moves_ref[g]) + dot_nn(low, moves_ref[g])

    quarter, part = quarter_sum.shape[0], quarter_sum.shape[0] // nc
    quarter_out[...] = folded[...].astype(BF16).reshape(nr, quarter, feats)
    wave = []
    for i in range(1, nr):
        to = ahead(i, 0)
        wave.append(push(quarter_out.at[to[0]], quarter_in.at[i - 1], fold_sems.at[0], i, to))
    send_tiles(4)

    def outer(i, _):
        y = i * step
        acc = jnp.zeros((area, feats), F32)
        for ky in range(3):
            acc += dot_nt(win_h_ref[pl.ds(y + ky, step)].reshape(area, 3 * feats), lanes_ref[1, ky])
        out_ref[pl.ds(y, step)] = (acc * masked(y)).astype(BF16).reshape(step, breadth, feats)
        return 0

    lax.fori_loop(0, height // step, outer, 0)

    for copy in wave:
        copy.wait()
    summed = quarter_out[r].astype(F32)
    for i in range(1, nr):
        summed += quarter_in[i - 1].astype(F32)
    quarter_sum[...] = summed
    for j in range(nc):
        part_out[j, :part] = quarter_sum[j * part : (j + 1) * part]
    wave = []
    for j in range(1, nc):
        to = ahead(0, j)
        wave.append(push(part_out.at[to[1]], part_in.at[j - 1], fold_sems.at[1], j, to))
    send_tiles(4)

    def lower(k, _):
        high, low = split(kept[2 * k] + kept[2 * k + 1])
        low_grad_ref[k] = (dot_nn(halve, high) + dot_nn(halve, low)).astype(BF16)
        return 0

    lax.fori_loop(0, height // 2, lower, 0, unroll=2)
    for copy in wave:
        copy.wait()
    share = part_out[c]
    for j in range(1, nc):
        share += part_in[j - 1]
    part_sum[...] = share
    part_all[c] = share
    wave = []
    for j in range(1, nc):
        wave.append(push(part_sum, part_all.at[c], fold_sems.at[2], j, ahead(0, j)))
    send_tiles(4)
    for copy in wave:
        copy.wait()
    for j in range(nc):
        quarter_sum[j * part : (j + 1) * part] = part_all[j, :part]
    rounded = quarter_sum[...].astype(BF16)
    near[...] = rounded
    sums_ref[r] = rounded
    wave = []
    for i in range(1, nr):
        wave.append(push(near, sums_ref.at[r], fold_sems.at[3], i, ahead(i, 0)))
    send_tiles(32)
    for copy in wave:
        copy.wait()
    for copy in late:
        copy.wait()


def whole(sizes, low, skip, grad, tissue, base, moves, major, tiling, slots, source):
    nr, nc = sizes
    height, breadth, feats = skip.shape
    tile_rows, tile_cols = tissue.shape
    wide = (height + 2, breadth, 3 * feats)
    side = height // tile_rows
    blocks = (source.shape[0], side * side, feats)
    lines = 18 * feats // G
    unit = nc * 16 // math.gcd(nc, 16)
    quarter = -(-lines // (nr * unit)) * unit
    part = quarter // nc
    padded = -(-part // 8) * 8
    vmem = pl.BlockSpec(memory_space=pltpu.VMEM)
    return pl.pallas_call(
        functools.partial(whole_kernel, sizes),
        out_shape=(
            jax.ShapeDtypeStruct(skip.shape, BF16),
            jax.ShapeDtypeStruct(low.shape, BF16),
            jax.ShapeDtypeStruct(blocks, BF16),
            jax.ShapeDtypeStruct(slots.shape, F32),
            jax.ShapeDtypeStruct((nr, quarter, feats), BF16),
        ),
        in_specs=[vmem] * 9 + [pl.BlockSpec(memory_space=pltpu.SMEM)],
        out_specs=(vmem,) * 5,
        scratch_shapes=[
            pltpu.VMEM(blocks, BF16),
            pltpu.VMEM(wide, BF16),
            pltpu.VMEM(wide, BF16),
            pltpu.VMEM(skip.shape, BF16),
            pltpu.VMEM(skip.shape, BF16),
            pltpu.VMEM((2, 3, feats, 3 * feats), BF16),
            pltpu.VMEM((tile_rows, breadth, feats), F32),
            pltpu.VMEM((2, 2, height, breadth, feats), BF16),
            pltpu.VMEM((2, 2, height, feats), F32),
            pltpu.VMEM((2, 2, 2, height, feats), BF16),
            pltpu.VMEM((2, 2, 2, breadth, feats), BF16),
            pltpu.VMEM((2, 2, 2, height, feats), BF16),
            pltpu.VMEM((2, 4, 2, 16, feats), BF16),
            pltpu.VMEM(wide, BF16),
            pltpu.VMEM(wide, BF16),
            pltpu.VMEM((18, feats, feats), BF16),
            pltpu.VMEM((2, 3, 3 * feats, feats), BF16),
            pltpu.VMEM((tile_rows * tile_cols, side * side, feats), BF16),
            pltpu.VMEM((2, height, feats), F32),
            pltpu.VMEM((2, 3, feats, 3 * feats), F32),
            pltpu.VMEM((lines, feats), F32),
            pltpu.VMEM((nr * quarter, feats), F32),
            pltpu.VMEM((nr, quarter, feats), BF16),
            pltpu.VMEM((nr - 1, quarter, feats), BF16),
            pltpu.VMEM((quarter, feats), F32),
            pltpu.VMEM((nc, padded, feats), F32),
            pltpu.VMEM((nc - 1, padded, feats), F32),
            pltpu.VMEM((padded, feats), F32),
            pltpu.VMEM((nc, padded, feats), F32),
            pltpu.VMEM((quarter, feats), BF16),
            pltpu.VMEM(skip.shape, F32),
            pltpu.SemaphoreType.DMA((2, 8)),
            pltpu.SemaphoreType.DMA((2, 8)),
            pltpu.SemaphoreType.DMA((2, nr * nc)),
            pltpu.SemaphoreType.DMA((2, nr * nc)),
            pltpu.SemaphoreType.DMA((4, 2, max(nr, nc))),
        ],
        compiler_params=pltpu.CompilerParams(
            collective_id=0, has_side_effects=True, vmem_limit_bytes=VMEM_BYTES
        ),
        name="whole",
    )(low, skip, grad, tissue, base, moves, major, tiling, slots, source)


def place_kernel(at_ref, got_ref, out_ref):
    def put(s, _):
        out_ref[s] = got_ref[at_ref[s]]
        return 0

    lax.fori_loop(0, out_ref.shape[0], put, 0, unroll=8)


def place(at, got):
    vmem = pl.BlockSpec(memory_space=pltpu.VMEM)
    return pl.pallas_call(
        place_kernel,
        out_shape=jax.ShapeDtypeStruct((at.shape[0],) + got.shape[1:], BF16),
        in_specs=[pl.BlockSpec(memory_space=pltpu.SMEM), vmem],
        out_specs=vmem,
        compiler_params=pltpu.CompilerParams(vmem_limit_bytes=VMEM_BYTES),
        name="place",
    )(at, got)


def on_device(sizes, low_feats, skip_feats, tissue_mask, owner_slot, filter_one, filter_two, out_grad):
    count = sizes[0] * sizes[1]
    height, breadth, feats = skip_feats.shape
    tile_rows, tile_cols = tissue_mask.shape
    tile_count = tile_rows * tile_cols
    side = height // tile_rows
    chans = feats // G
    per_owner = 2 * tile_count // count

    moves = jnp.asarray(feature_moves(feats), BF16)
    major = jnp.asarray(element_major(feats), BF16)
    tiling = jnp.asarray(tile_order(side, breadth), BF16)
    base = jnp.stack([filter_one, filter_two]).reshape(2, chans, 9, feats)
    base = base.transpose(0, 2, 1, 3).reshape(18 * chans, feats)

    slot_list = owner_slot.reshape(-1)
    owner, local = slot_list // tile_count, slot_list % tile_count
    before = (owner[:, None] == owner[None, :]) & (local[None, :] < local[:, None])
    position = owner * per_owner + jnp.sum(before.astype(jnp.int32), axis=1)
    picked = position[None, :] == jnp.arange(count * per_owner, dtype=jnp.int32)[:, None]
    numbers = jnp.arange(tile_count, dtype=jnp.int32)
    source = jnp.sum(jnp.where(picked, numbers[None, :], 0), axis=1).astype(jnp.int32)
    send_slots = jnp.sum(jnp.where(picked, local[None, :] + 1, 0), axis=1).astype(jnp.int32)

    slots = jnp.broadcast_to(send_slots.astype(F32).reshape(count, per_owner, 1), (count, per_owner, 128))
    slots = jnp.pad(slots, ((0, 0), (0, -per_owner % 8), (0, 0)))
    output, low_grad, got, got_slots, sums = whole(
        sizes, low_feats, skip_feats, out_grad, tissue_mask, base, moves, major, tiling, slots, source
    )
    scale = 1.0 / math.sqrt(height * breadth * count)
    lines = 18 * chans
    grads = sums.astype(F32).reshape(-1, feats)[:lines].reshape(2, 9, chans, feats) * scale
    grads = grads.transpose(0, 2, 1, 3).reshape(2, chans, 3, 3, feats)

    got_slots = got_slots[:, :per_owner, 0].reshape(-1).astype(jnp.int32) - 1
    match = got_slots[None, :] == numbers[:, None]
    at = jnp.sum(jnp.where(match, jnp.arange(count * per_owner, dtype=jnp.int32)[None, :], 0), axis=1)
    skip_grad = place(at.astype(jnp.int32), got).reshape(tile_count, side, side, feats)
    return output, skip_grad, low_grad, grads[0], grads[1]


def solution(mesh):
    sizes = (mesh.shape["rows"], mesh.shape["cols"])
    block = P("rows", "cols", None)
    return jax.shard_map(
        functools.partial(on_device, sizes),
        mesh=mesh,
        in_specs=(block, block, P("rows", "cols"), P("rows", "cols"), P(), P(), block),
        out_specs=(block, P(("rows", "cols"), None, None, None), block, P(), P()),
        check_vma=False,
    )
```

```python
import functools
import math

import jax
import jax.numpy as jnp
import numpy as np
from jax import lax
from jax.experimental import pallas as pl
from jax.experimental.pallas import tpu as pltpu
from jax.sharding import PartitionSpec as P

G = 8
MESH = pl.DeviceIdType.MESH
F32 = jnp.float32
BF16 = jnp.bfloat16
VMEM_BYTES = 56 * 1024 * 1024


def element_inverse(element):
    mirror, turns = element // 4, element % 4
    return element if mirror else (4 - turns) % 4


def element_product(first, second):
    mirror = (first // 4 + second // 4) % 2
    turns = (first % 4 + (1 - 2 * (first // 4)) * (second % 4)) % 4
    return mirror * 4 + turns


def element_act(element, row_off, col_off):
    mirror, turns = element // 4, element % 4
    row_now, col_now = row_off, -col_off if mirror else col_off
    for _ in range(turns):
        row_now, col_now = -col_now, row_now
    return row_now, col_now


def cell_source(element, cell):
    row, col = element_act(element_inverse(element), cell // 3 - 1, cell % 3 - 1)
    return (row + 1) * 3 + col + 1


def feature_moves(features):
    moves = np.zeros((G, features, features), np.float32)
    for elem in range(G):
        for i in range(features):
            moves[elem, i, i // G * G + element_product(element_inverse(elem), i % G)] = 1
    return moves


def element_major(features):
    channels = features // G
    order = np.zeros((features, features), np.float32)
    for o in range(channels):
        for g in range(G):
            order[g * channels + o, o * G + g] = 1
    return order


def tile_order(side, breadth):
    order = np.zeros((side * breadth, side * breadth), np.float32)
    for py in range(side):
        for x in range(breadth):
            order[(x // side * side + py) * side + x % side, py * breadth + x] = 1
    return order


def dot_nn(a, b):
    return lax.dot_general(a, b, (((1,), (0,)), ((), ())), preferred_element_type=F32)


def dot_nt(a, b):
    return lax.dot_general(a, b, (((1,), (1,)), ((), ())), preferred_element_type=F32)


def split(value):
    high = value.astype(BF16)
    return high, (value - high.astype(F32)).astype(BF16)


def shifted(row, left, right):
    breadth = row.shape[0]
    at = lax.broadcasted_iota(jnp.int32, row.shape, 0)
    before = jnp.where(at == 0, left, pltpu.roll(row, 1, 0))
    after = jnp.where(at == breadth - 1, right, pltpu.roll(row, breadth - 1, 0))
    return before.astype(BF16), after.astype(BF16)


def whole_kernel(
    shape,
    low_ref, skip_ref, grad_ref, tissue_ref, base_ref, moves_ref, major_ref, tiling_ref, slots_ref, from_ref,
    out_ref, low_grad_ref, got_ref, at_ref, sums_ref,
    got_slots_ref, send_ref, win_m_ref, win_h_ref, two_ref, pre_ref, lanes_ref, mask_ref,
    field, ends, wire, got_row, got_col, got_cor, win_g, win_p, gathered, rows_ref, tiles, halo32,
    total, lined, folded, quarter_out, quarter_in, quarter_sum, stage, part_out, part_in, part_sum, part_all,
    near, kept, send_sem, recv_sem, tile_sem, slot_sem, fold_sems,
):
    nr, nc = shape
    count = nr * nc
    height, breadth, feats = skip_ref.shape
    tile_rows, tile_cols = tissue_ref.shape
    side = height // tile_rows
    chans = feats // G
    r, c = lax.axis_index("rows"), lax.axis_index("cols")
    me = r * nc + c
    up, down = lax.rem(r + nr - 1, nr), lax.rem(r + 1, nr)
    west, east = lax.rem(c + nc - 1, nc), lax.rem(c + 1, nc)
    around = ((up, c), (down, c), (r, west), (r, east), (up, west), (up, east), (down, west), (down, east))

    def ahead(i, j):
        return lax.rem(r + i, nr), lax.rem(c + j, nc)

    offsets = sorted(
        (i, j) for i in range(nr) for j in range(nc) if i or j
    )

    barrier = pltpu.get_barrier_semaphore()
    for i, j in offsets:
        pl.semaphore_signal(barrier, inc=1, device_id=ahead(i, j), device_id_type=MESH)

    spread = (
        lax.broadcasted_iota(jnp.int32, (breadth, tile_cols), 0) // side
        == lax.broadcasted_iota(jnp.int32, (breadth, tile_cols), 1)
    )
    ones = jnp.ones((tile_cols, feats), BF16)
    for tr in range(tile_rows):
        held = jnp.where(spread, tissue_ref[tr : tr + 1, :].astype(F32), 0.0).astype(BF16)
        mask_ref[tr] = dot_nn(held, ones)

    double = (
        lax.broadcasted_iota(jnp.int32, (breadth, breadth // 2), 0) // 2
        == lax.broadcasted_iota(jnp.int32, (breadth, breadth // 2), 1)
    ).astype(F32).astype(BF16)

    def enter(pair, _):
        raised = dot_nn(double, low_ref[pair])
        mask = mask_ref[pair * 2 // side]
        for k in range(2):
            y = pair * 2 + k
            merged = (raised + skip_ref[y].astype(F32)) * mask
            two = grad_ref[y].astype(F32) * mask
            field[0, 0, y] = merged.astype(BF16)
            field[0, 1, y] = two.astype(BF16)
            two_ref[y] = two.astype(BF16)
            for f, value in enumerate((merged, two)):
                ends[0, f, pl.ds(y, 1), :] = value[0:1]
                ends[1, f, pl.ds(y, 1), :] = value[breadth - 1 : breadth]
        return 0

    lax.fori_loop(0, height // 2, enter, 0, unroll=2)

    def copies(ph):
        low_end, high_end = pl.ds(0, 16), pl.ds(breadth - 16, 16)
        plan = (
            (field.at[ph, :, 0], got_row.at[ph, 1]),
            (field.at[ph, :, height - 1], got_row.at[ph, 0]),
            (wire.at[ph, 0], got_col.at[ph, 1]),
            (wire.at[ph, 1], got_col.at[ph, 0]),
            (field.at[ph, :, 0, low_end], got_cor.at[ph, 3]),
            (field.at[ph, :, 0, high_end], got_cor.at[ph, 2]),
            (field.at[ph, :, height - 1, low_end], got_cor.at[ph, 1]),
            (field.at[ph, :, height - 1, high_end], got_cor.at[ph, 0]),
        )
        return [
            pltpu.make_async_remote_copy(
                src_ref=src, dst_ref=dst, send_sem=send_sem.at[ph, k], recv_sem=recv_sem.at[ph, k],
                device_id=around[k], device_id_type=MESH,
            )
            for k, (src, dst) in enumerate(plan)
        ]

    def send_halo(ph):
        wire[ph] = ends[...].astype(BF16)
        started = copies(ph)
        for copy in started:
            copy.start()
        return started

    in_up = jnp.where(r > 0, 1.0, 0.0)
    in_down = jnp.where(r < nr - 1, 1.0, 0.0)
    in_west = jnp.where(c > 0, 1.0, 0.0)
    in_east = jnp.where(c < nc - 1, 1.0, 0.0)

    def put(out, y, row, left, right):
        before, after = shifted(row, left, right)
        out[y, :, 0:feats] = before
        out[y, :, feats : 2 * feats] = row.astype(BF16)
        out[y, :, 2 * feats : 3 * feats] = after

    def inner(ph, f, out):
        def line(y, _):
            put(out, y + 1, field[ph, f, y].astype(F32), 0.0, 0.0)
            return 0

        lax.fori_loop(0, height, line, 0, unroll=4)

    def border(ph, f, out):
        halo32[0] = got_col[ph, 0, f].astype(F32) * in_west
        halo32[1] = got_col[ph, 1, f].astype(F32) * in_east
        at = lax.broadcasted_iota(jnp.int32, (16, feats), 0)

        def line(y, _):
            left = out[y + 1, 0:16, 0:feats].astype(F32)
            out[y + 1, 0:16, 0:feats] = jnp.where(at == 0, halo32[0, pl.ds(y, 1), :], left).astype(BF16)
            right = out[y + 1, breadth - 16 : breadth, 2 * feats : 3 * feats].astype(F32)
            out[y + 1, breadth - 16 : breadth, 2 * feats : 3 * feats] = jnp.where(
                at == 15, halo32[1, pl.ds(y, 1), :], right
            ).astype(BF16)
            return 0

        lax.fori_loop(0, height, line, 0, unroll=4)
        for k, (y, gate) in enumerate(((0, in_up), (height + 1, in_down))):
            row = got_row[ph, k, f].astype(F32) * gate
            left = got_cor[ph, 2 * k, f].astype(F32)[15:16] * (gate * in_west)
            right = got_cor[ph, 2 * k + 1, f].astype(F32)[0:1] * (gate * in_east)
            put(out, y, row, left, right)

    pl.semaphore_wait(barrier, count - 1)
    first = send_halo(0)

    def push(src, dst, sems, k, device):
        copy = pltpu.make_async_remote_copy(
            src_ref=src, dst_ref=dst, send_sem=sems.at[0, k], recv_sem=sems.at[1, k],
            device_id=device, device_id_type=MESH,
        )
        copy.start()
        return copy

    late = []
    for k, (i, j) in enumerate(offsets):
        to = ahead(i, j)
        late.append(push(slots_ref.at[to[0] * nc + to[1]], got_slots_ref.at[me], slot_sem, k, to))
    got_slots_ref[me] = slots_ref[me]

    def gather(g):
        placed = dot_nt(base_ref[...], moves_ref[g]).astype(BF16)
        for f in range(2):
            for cell in range(9):
                at = (f * 9 + cell_source(g, cell)) * chans
                gathered[f * 9 + cell, g * chans : (g + 1) * chans, :] = placed[at : at + chans]

    for g in range(G):
        gather(g)
    for f in range(2):
        for ky in range(3):
            for kx in range(3):
                full = lax.dot_general(
                    major_ref[...], gathered[f * 9 + ky * 3 + kx], (((0,), (0,)), ((), ())),
                    preferred_element_type=F32,
                ).astype(BF16)
                lanes_ref[f, ky, :, kx * feats : (kx + 1) * feats] = full
                rows_ref[f, 2 - ky, (2 - kx) * feats : (3 - kx) * feats, :] = full

    inner(0, 0, win_m_ref)
    inner(0, 1, win_g)
    for copy in first:
        copy.wait()
    border(0, 0, win_m_ref)
    border(0, 1, win_g)

    step = 2 * side
    area = step * breadth

    def masked(y):
        two_rows = mask_ref[pl.ds(y // side, 2)]
        return jnp.broadcast_to(two_rows[:, None], (2, side, breadth, feats)).reshape(area, feats)

    def middle(i, _):
        y = i * step
        pre = jnp.zeros((area, feats), F32)
        back = jnp.zeros((area, feats), F32)
        for ky in range(3):
            pre += dot_nt(win_m_ref[pl.ds(y + ky, step)].reshape(area, 3 * feats), lanes_ref[0, ky])
            back += dot_nn(win_g[pl.ds(y + ky, step)].reshape(area, 3 * feats), rows_ref[1, ky])
        mask = masked(y)
        sigma = jax.nn.sigmoid(pre)
        hidden = (pre * sigma * mask).reshape(step, breadth, feats)
        slope = (back * (sigma * (1.0 + pre * (1.0 - sigma))) * mask).reshape(step, breadth, feats)
        for f, value in enumerate((hidden, slope)):
            field[1, f, pl.ds(y, step)] = value.astype(BF16)
            for k in range(step):
                ends[0, f, pl.ds(y + k, 1), :] = value[k, 0:1]
                ends[1, f, pl.ds(y + k, 1), :] = value[k, breadth - 1 : breadth]
        pre_ref[pl.ds(y, step)] = slope.astype(BF16)
        return 0

    lax.fori_loop(0, height // step, middle, 0)
    second = send_halo(1)

    def terms(f, grads, window):
        total[f] = jnp.zeros(total.shape[1:], F32)

        def add(i, _):
            y = i * step
            turned = dot_nt(major_ref[...], grads[pl.ds(y, step)].reshape(area, feats)).astype(BF16)
            for ky in range(3):
                total[f, ky] += dot_nn(turned, window[pl.ds(y + ky, step)].reshape(area, 3 * feats))
            return 0

        lax.fori_loop(0, height // step, add, 0)

    inner(1, 1, win_p)
    inner(1, 0, win_h_ref)
    for copy in second:
        copy.wait()
    border(1, 1, win_p)

    halve = (
        lax.broadcasted_iota(jnp.int32, (breadth // 2, breadth), 1) // 2
        == lax.broadcasted_iota(jnp.int32, (breadth // 2, breadth), 0)
    ).astype(F32).astype(BF16)

    def last(i, _):
        y = i * step
        total = jnp.zeros((area, feats), F32)
        for ky in range(3):
            total += dot_nn(win_p[pl.ds(y + ky, step)].reshape(area, 3 * feats), rows_ref[0, ky])
        total = total * masked(y)
        for t in range(2):
            rows = total[t * side * breadth : (t + 1) * side * breadth]
            placed = dot_nn(tiling_ref[...], rows.astype(BF16)).astype(BF16)
            tiles[pl.ds((i * 2 + t) * tile_cols, tile_cols)] = placed.reshape(tile_cols, side * side, feats)
        kept[pl.ds(y, step)] = total.reshape(step, breadth, feats)
        return 0

    lax.fori_loop(0, height // step, last, 0)

    each = send_ref.shape[0] // count

    def pick(to):
        base = (to[0] * nc + to[1]) * each
        for q in range(each):
            send_ref[base + q] = tiles[from_ref[base + q]]
        return pl.ds(base, each)

    turn = lax.rem(r, 2) * (nc // 2) + (r // 2) * (nc // 4)
    queue = [(i, lax.rem(turn + j, nc)) for i in range(1, nr) for j in range(nc)]
    queue += [(0, 1 + lax.rem(turn + j, nc - 1)) for j in range(nc - 1)]

    def send_tiles(part_of):
        for _ in range(min(len(queue), len(offsets) * part_of // 32 + 1)):
            i, j = queue.pop(0)
            to = ahead(i, j)
            blocks = pick(to)
            late.append(push(send_ref.at[blocks], got_ref.at[pl.ds(me * each, each)], tile_sem, i * nc + j, to))

    send_tiles(15)
    own = pick((r, c))
    got_ref[own] = send_ref[own]

    border(1, 0, win_h_ref)
    terms(0, pre_ref, win_m_ref)
    terms(1, two_ref, win_h_ref)

    folded[...] = jnp.zeros_like(folded)
    lines = 18 * chans
    for g in range(G):
        for f in range(2):
            for cell in range(9):
                at = (f * 9 + cell_source(g, cell)) * chans
                ky, kx = cell // 3, cell % 3
                lined[at : at + chans, :] = total[
                    f, ky, g * chans : (g + 1) * chans, kx * feats : (kx + 1) * feats
                ]
        high, low = split(lined[...])
        folded[:lines] += dot_nn(high, moves_ref[g]) + dot_nn(low, moves_ref[g])

    quarter, part = quarter_sum.shape[0], quarter_sum.shape[0] // nc
    quarter_out[...] = folded[...].astype(BF16).reshape(nr, quarter, feats)
    wave = []
    for i in range(1, nr):
        to = ahead(i, 0)
        wave.append(push(quarter_out.at[to[0]], quarter_in.at[i - 1], fold_sems.at[0], i, to))
    send_tiles(3)

    def outer(i, _):
        y = i * step
        acc = jnp.zeros((area, feats), F32)
        for ky in range(3):
            acc += dot_nt(win_h_ref[pl.ds(y + ky, step)].reshape(area, 3 * feats), lanes_ref[1, ky])
        out_ref[pl.ds(y, step)] = (acc * masked(y)).astype(BF16).reshape(step, breadth, feats)
        return 0

    lax.fori_loop(0, height // step, outer, 0)

    for copy in wave:
        copy.wait()
    summed = quarter_out[r].astype(F32)
    for i in range(1, nr):
        summed += quarter_in[i - 1].astype(F32)
    quarter_sum[...] = summed
    for j in range(nc):
        for h in range(feats // 128):
            stage[j, h * part : (h + 1) * part] = quarter_sum[
                j * part : (j + 1) * part, h * 128 : (h + 1) * 128
            ]
    part_out[...] = stage[...].astype(BF16)
    wave = []
    for j in range(1, nc):
        to = ahead(0, j)
        wave.append(push(part_out.at[to[1]], part_in.at[j - 1], fold_sems.at[1], j, to))
    send_tiles(3)

    def lower(k, _):
        high, low = split(kept[2 * k] + kept[2 * k + 1])
        low_grad_ref[k] = (dot_nn(halve, high) + dot_nn(halve, low)).astype(BF16)
        return 0

    lax.fori_loop(0, height // 2, lower, 0, unroll=2)
    for copy in wave:
        copy.wait()
    share = part_out[c].astype(F32)
    for j in range(1, nc):
        share += part_in[j - 1].astype(F32)
    part_sum[...] = share.astype(BF16)
    part_all[c] = share.astype(BF16)
    wave = []
    for j in range(1, nc):
        wave.append(push(part_sum, part_all.at[c], fold_sems.at[2], j, ahead(0, j)))
    send_tiles(3)
    for copy in wave:
        copy.wait()
    stage[...] = part_all[...].astype(F32)
    for j in range(nc):
        for h in range(feats // 128):
            quarter_sum[j * part : (j + 1) * part, h * 128 : (h + 1) * 128] = stage[
                j, h * part : (h + 1) * part
            ]
    rounded = quarter_sum[...].astype(BF16)
    near[...] = rounded
    sums_ref[r] = rounded
    wave = []
    for i in range(1, nr):
        wave.append(push(near, sums_ref.at[r], fold_sems.at[3], i, ahead(i, 0)))
    send_tiles(32)
    for copy in wave:
        copy.wait()
    for copy in late:
        copy.wait()
    found = got_slots_ref[...]
    axis = [lax.broadcasted_iota(jnp.int32, found.shape, d) for d in range(3)]
    hit = found == (axis[2] + 1).astype(F32)
    at = jnp.where(hit, (axis[0] * each + axis[1]).astype(F32), 0.0)
    at = jnp.sum(at.reshape(-1, found.shape[2]), axis=0, keepdims=True)
    at_ref[...] = jnp.broadcast_to(at, at_ref.shape).astype(jnp.int32)


def whole(sizes, low, skip, grad, tissue, base, moves, major, tiling, slots, source):
    nr, nc = sizes
    height, breadth, feats = skip.shape
    tile_rows, tile_cols = tissue.shape
    wide = (height + 2, breadth, 3 * feats)
    side = height // tile_rows
    blocks = (source.shape[0], side * side, feats)
    lines = 18 * feats // G
    unit = nc * 16 // math.gcd(nc, 16)
    quarter = -(-lines // (nr * unit)) * unit
    part = quarter // nc
    packed = (-(-part * (feats // 128) // 16) * 16, 128)
    vmem = pl.BlockSpec(memory_space=pltpu.VMEM)
    return pl.pallas_call(
        functools.partial(whole_kernel, sizes),
        out_shape=(
            jax.ShapeDtypeStruct(skip.shape, BF16),
            jax.ShapeDtypeStruct(low.shape, BF16),
            jax.ShapeDtypeStruct(blocks, BF16),
            jax.ShapeDtypeStruct((8, slots.shape[2]), jnp.int32),
            jax.ShapeDtypeStruct((nr, quarter, feats), BF16),
        ),
        in_specs=[vmem] * 9 + [pl.BlockSpec(memory_space=pltpu.SMEM)],
        out_specs=(vmem,) * 5,
        scratch_shapes=[
            pltpu.VMEM(slots.shape, F32),
            pltpu.VMEM(blocks, BF16),
            pltpu.VMEM(wide, BF16),
            pltpu.VMEM(wide, BF16),
            pltpu.VMEM(skip.shape, BF16),
            pltpu.VMEM(skip.shape, BF16),
            pltpu.VMEM((2, 3, feats, 3 * feats), BF16),
            pltpu.VMEM((tile_rows, breadth, feats), F32),
            pltpu.VMEM((2, 2, height, breadth, feats), BF16),
            pltpu.VMEM((2, 2, height, feats), F32),
            pltpu.VMEM((2, 2, 2, height, feats), BF16),
            pltpu.VMEM((2, 2, 2, breadth, feats), BF16),
            pltpu.VMEM((2, 2, 2, height, feats), BF16),
            pltpu.VMEM((2, 4, 2, 16, feats), BF16),
            pltpu.VMEM(wide, BF16),
            pltpu.VMEM(wide, BF16),
            pltpu.VMEM((18, feats, feats), BF16),
            pltpu.VMEM((2, 3, 3 * feats, feats), BF16),
            pltpu.VMEM((tile_rows * tile_cols, side * side, feats), BF16),
            pltpu.VMEM((2, height, feats), F32),
            pltpu.VMEM((2, 3, feats, 3 * feats), F32),
            pltpu.VMEM((lines, feats), F32),
            pltpu.VMEM((nr * quarter, feats), F32),
            pltpu.VMEM((nr, quarter, feats), BF16),
            pltpu.VMEM((nr - 1, quarter, feats), BF16),
            pltpu.VMEM((quarter, feats), F32),
            pltpu.VMEM((nc,) + packed, F32),
            pltpu.VMEM((nc,) + packed, BF16),
            pltpu.VMEM((nc - 1,) + packed, BF16),
            pltpu.VMEM(packed, BF16),
            pltpu.VMEM((nc,) + packed, BF16),
            pltpu.VMEM((quarter, feats), BF16),
            pltpu.VMEM(skip.shape, F32),
            pltpu.SemaphoreType.DMA((2, 8)),
            pltpu.SemaphoreType.DMA((2, 8)),
            pltpu.SemaphoreType.DMA((2, nr * nc)),
            pltpu.SemaphoreType.DMA((2, nr * nc)),
            pltpu.SemaphoreType.DMA((4, 2, max(nr, nc))),
        ],
        compiler_params=pltpu.CompilerParams(
            collective_id=0, has_side_effects=True, vmem_limit_bytes=VMEM_BYTES
        ),
        name="whole",
    )(low, skip, grad, tissue, base, moves, major, tiling, slots, source)


def place_kernel(at_ref, got_ref, out_ref):
    def put(s, _):
        out_ref[s] = got_ref[at_ref[0, s]]
        return 0

    lax.fori_loop(0, out_ref.shape[0], put, 0, unroll=8)


def place(at, got):
    vmem = pl.BlockSpec(memory_space=pltpu.VMEM)
    return pl.pallas_call(
        place_kernel,
        out_shape=jax.ShapeDtypeStruct((at.shape[1],) + got.shape[1:], BF16),
        in_specs=[pl.BlockSpec(memory_space=pltpu.SMEM), vmem],
        out_specs=vmem,
        compiler_params=pltpu.CompilerParams(vmem_limit_bytes=VMEM_BYTES),
        name="place",
    )(at, got)


def on_device(sizes, low_feats, skip_feats, tissue_mask, owner_slot, filter_one, filter_two, out_grad):
    count = sizes[0] * sizes[1]
    height, breadth, feats = skip_feats.shape
    tile_rows, tile_cols = tissue_mask.shape
    tile_count = tile_rows * tile_cols
    side = height // tile_rows
    chans = feats // G
    per_owner = 2 * tile_count // count

    moves = jnp.asarray(feature_moves(feats), BF16)
    major = jnp.asarray(element_major(feats), BF16)
    tiling = jnp.asarray(tile_order(side, breadth), BF16)
    base = jnp.stack([filter_one, filter_two]).reshape(2, chans, 9, feats)
    base = base.transpose(0, 2, 1, 3).reshape(18 * chans, feats)

    slot_list = owner_slot.reshape(-1)
    owner, local = slot_list // tile_count, slot_list % tile_count
    before = (owner[:, None] == owner[None, :]) & (local[None, :] < local[:, None])
    position = owner * per_owner + jnp.sum(before.astype(jnp.int32), axis=1)
    picked = position[None, :] == jnp.arange(count * per_owner, dtype=jnp.int32)[:, None]
    numbers = jnp.arange(tile_count, dtype=jnp.int32)
    source = jnp.sum(jnp.where(picked, numbers[None, :], 0), axis=1).astype(jnp.int32)
    send_slots = jnp.sum(jnp.where(picked, local[None, :] + 1, 0), axis=1).astype(jnp.int32)

    slots = jnp.broadcast_to(send_slots.astype(F32).reshape(count, per_owner, 1), (count, per_owner, tile_count))
    slots = jnp.pad(slots, ((0, 0), (0, -per_owner % 8), (0, 0)))
    output, low_grad, got, at, sums = whole(
        sizes, low_feats, skip_feats, out_grad, tissue_mask, base, moves, major, tiling, slots, source
    )
    scale = 1.0 / math.sqrt(height * breadth * count)
    lines = 18 * chans
    grads = sums.astype(F32).reshape(-1, feats)[:lines].reshape(2, 9, chans, feats) * scale
    grads = grads.transpose(0, 2, 1, 3).reshape(2, chans, 3, 3, feats)

    skip_grad = place(at, got).reshape(tile_count, side, side, feats)
    return output, skip_grad, low_grad, grads[0], grads[1]


def solution(mesh):
    sizes = (mesh.shape["rows"], mesh.shape["cols"])
    block = P("rows", "cols", None)
    return jax.shard_map(
        functools.partial(on_device, sizes),
        mesh=mesh,
        in_specs=(block, block, P("rows", "cols"), P("rows", "cols"), P(), P(), block),
        out_specs=(block, P(("rows", "cols"), None, None, None), block, P(), P()),
        check_vma=False,
    )
```
